512 devices in a mesh: space: 16 (over z, core), member: 8 (over y), tm: 4 (over x).
Axes of the slice: x: 4, y: 8, z: 8, core: 2. Of those that a mesh axis runs over, the one named last changes fastest.
Arguments:
- ens_pert: bfloat16 [8, 128, 131072], P('tm', 'member', 'space'), may hold values from -6 to 6
- weights: float32 [128, 512], P('member', 'space'), may hold values from -6 to 6
- foot_block: int32 [8, 16, 16, 8, 32], P('tm', 'space'), may hold values from 0 to 31
- foot_offset: int32 [8, 16, 16, 8, 32], P('tm', 'space'), may hold values from 0 to 255
- innovation: float32 [8, 16, 8, 16, 32], P('tm', 'space', 'member'), may hold values from -6 to 6
- inv_var: float32 [8, 16, 8, 16, 32], P('tm', 'space', 'member'), may hold values from 0.25 to 2.5
- obs_count: int32 [8, 16, 8, 16], P('tm', 'space', 'member'), may hold values from 1 to 32, as said below
Outputs:
- gradient: float32 [128, 512], P('member', 'space')
The draws below stay inside these ranges and needn't reach their ends.
Inputs may be any that keep to these rules, and one draw needn't show every extreme that they name: `obs_count`: live slots come first among the 32 slots; in every time slot one destination tile has all 32 slots live from every owner.
All inputs are finite; a program needn't handle non-finite values.
Results may differ from the reference program's by a relative error of at most 0.0029.
Values sent between devices are 32-bit elements; how exact they have to be, the bound alone decides.
No kernel may reach another device: no remote copies, remote signals or barrier semaphores. Data moves between devices by JAX's collectives and lax.ppermute only.
A program may use at most 64 MiB of HBM per device.

```python
import math
import jax
import jax.numpy as jnp
from jax import lax

CELL_DEV = 8192
BLOCK = 256
CAP = 32
TILES = 16
GROUPS = 8
MEMBERS = 128
TIMES = 8
BLK_DEV = 32
BLOCKS = 512
CELLS = 131072


def draw_obs_count(key, part):
    first_key, second_key = jax.random.split(key)
    base_count = jax.random.randint(first_key, (TIMES, TILES, GROUPS, TILES), 1, CAP + 1).astype(jnp.int32)
    hot_tile = jax.random.randint(second_key, (TIMES,), 0, TILES).astype(jnp.int32)
    dest_index = jnp.arange(TILES).astype(jnp.int32)
    is_hot = dest_index[None, None, None, :] == hot_tile[:, None, None, None]
    return jnp.where(is_hot, jnp.int32(CAP), base_count).astype(jnp.int32)


def with_ends(entries, own_key, smallest, high):
    extent = entries.shape
    place = [jax.random.randint(jax.random.fold_in(own_key, axis), (), 0, extent[axis]) for axis in range(len(extent))]
    entries = entries.at[tuple(place)].set(smallest)
    longest = extent.index(max(extent))
    place[longest] = (place[longest] + 1) % extent[longest]
    return entries.at[tuple(place)].set(high)


def block_levels(key, shape, cuts, least, top_value):
    loudness, own = 1.0, jax.random.fold_in(key, 6)
    for position, blocks in cuts:
        draws = jnp.exp(jax.random.uniform(jax.random.fold_in(own, position), (blocks,), jnp.float32, least / len(cuts), top_value / len(cuts)))
        loudness = loudness * jnp.repeat(draws, shape[position] // blocks).reshape([-1 if axis == position else 1 for axis in range(len(shape))])
    return loudness


def centred(key, dims, width, most, cuts=(), held_as=jnp.bfloat16):
    gain = block_levels(key, dims, cuts, -0.22, 0.18) if cuts else 1.0
    entries = jax.random.normal(key, dims, jnp.float32) * width * gain
    return jnp.minimum(jnp.maximum(entries, -most), most).astype(held_as)


def setup_inputs(seed: int = 0) -> dict:
    streams_of = jax.random.split(jax.random.key(seed), 8)
    return {
        "ens_pert": centred(streams_of[0], (TIMES, MEMBERS, CELLS), 1.0, 6.0, ((0, 4), (1, 8), (2, 16))),
        "weights": centred(streams_of[1], (MEMBERS, BLOCKS), 1.0, 6.0, ((0, 8), (1, 16)), jnp.float32),
        "foot_block": with_ends(jax.random.randint(streams_of[2], (TIMES, TILES, TILES, GROUPS, CAP), 0, BLK_DEV), jax.random.fold_in(streams_of[2], 1), 0, BLK_DEV - 1).astype(jnp.int32),
        "foot_offset": with_ends(jax.random.randint(streams_of[3], (TIMES, TILES, TILES, GROUPS, CAP), 0, BLOCK), jax.random.fold_in(streams_of[3], 1), 0, BLOCK - 1).astype(jnp.int32),
        "innovation": centred(streams_of[4], (TIMES, TILES, GROUPS, TILES, CAP), 1.0, 6.0, ((0, 4), (1, 16), (2, 8)), jnp.float32),
        "inv_var": jnp.clip(jnp.exp(math.log(2.5) - 2.3025851 * jax.random.uniform(streams_of[5], (TIMES, TILES, GROUPS, TILES, CAP), jnp.float32) ** block_levels(streams_of[5], (TIMES, TILES, GROUPS, TILES, CAP), ((0, 4), (1, 16), (2, 8)), -0.2, 0.2)), 0.25, 2.5),
        "obs_count": draw_obs_count(jax.random.fold_in(streams_of[7], 71), 0),
    }


def reference(ens_pert, weights, foot_block, foot_offset, innovation, inv_var, obs_count):
    norm_scale = 1.0 / math.sqrt(MEMBERS - 1)
    weights_rounded = lax.optimization_barrier(weights.astype(jnp.bfloat16)).astype(jnp.float32)

    def make_field(member_rows):
        shaped = member_rows.astype(jnp.float32).reshape(MEMBERS, BLOCKS, BLOCK)
        return jnp.einsum('mbc,mb->bc', shaped, weights_rounded, precision=lax.Precision.HIGHEST).reshape(CELLS)
    fields = norm_scale * lax.map(make_field, ens_pert)
    tile_start = (jnp.arange(TILES).astype(jnp.int32) * CELL_DEV).reshape(1, TILES, 1, 1, 1)
    cell_index = foot_block * BLOCK + foot_offset + tile_start
    flat_index = cell_index.reshape(TIMES, -1)
    picked = jnp.take_along_axis(fields, flat_index, axis=1).reshape(cell_index.shape)
    model_obs = jnp.transpose(picked, (0, 2, 3, 1, 4))
    slot_index = jnp.arange(CAP).astype(jnp.int32)
    is_live = slot_index < obs_count[..., None]
    residual = jnp.where(is_live, inv_var * (model_obs - innovation), jnp.zeros_like(innovation))
    back = jnp.transpose(residual, (0, 3, 1, 2, 4)).reshape(TIMES, -1)
    time_start = (jnp.arange(TIMES).astype(jnp.int32) * CELLS)[:, None]
    adjoint = jax.ops.segment_sum(back.reshape(-1), (flat_index + time_start).reshape(-1), num_segments=TIMES * CELLS)
    adjoint = adjoint.reshape(TIMES, BLOCKS, BLOCK)
    adjoint = lax.optimization_barrier(adjoint.astype(jnp.bfloat16)).astype(jnp.float32)

    def slot_gradient(pair):
        member_rows, adjoint_slot = pair
        shaped = member_rows.astype(jnp.float32).reshape(MEMBERS, BLOCKS, BLOCK)
        return jnp.einsum('mbc,bc->mb', shaped, adjoint_slot, precision=lax.Precision.HIGHEST)
    summed = lax.optimization_barrier(jnp.sum(lax.map(slot_gradient, (ens_pert, adjoint)), axis=0))
    return weights + norm_scale * summed
```

```python
import math

import jax
import jax.numpy as jnp
from jax import lax
from jax.experimental import pallas as pl
from jax.experimental.pallas import tpu as pltpu
from jax.sharding import PartitionSpec as P

BLOCK = 256
VMEM = pl.BlockSpec(memory_space=pltpu.VMEM)
PARAMS = pltpu.CompilerParams(vmem_limit_bytes=32 * 1024 * 1024)
F32, BF16 = jnp.float32, jnp.bfloat16
NT = (((1,), (1,)), ((), ()))


def owned_kernel(innov_ref, var_ref, count_ref, out_ref):
    slots, tiles, cap = innov_ref.shape
    diag = lax.broadcasted_iota(jnp.int32, (tiles, tiles), 0) == lax.broadcasted_iota(
        jnp.int32, (tiles, tiles), 1
    )
    lane = lax.broadcasted_iota(jnp.int32, (tiles, cap), 1).astype(F32)
    for t in range(slots):
        row = count_ref[t : t + 1, :].astype(F32)
        column = jnp.sum(jnp.where(diag, row, 0.0), axis=1, keepdims=True)
        w = jnp.where(lane < column, var_ref[t], 0.0)
        out_ref[:, t * cap : (t + 1) * cap] = w
        out_ref[:, (slots + t) * cap : (slots + t + 1) * cap] = w * innov_ref[t]


def pick_kernel(scale, ens_ref, w_ref, fb_ref, fo_ref, pick_ref, fbr_ref, for_ref, field, split):
    slots, members, cells = ens_ref.shape
    blocks = cells // BLOCK
    tiles, groups, cap = fb_ref.shape[1:]
    quarters = 128 // cap
    a_rows = tiles // quarters
    for t in range(slots):
        for a in range(tiles):
            rows = pl.ds((t * a_rows + a % a_rows) * groups, groups)
            lanes = slice((a // a_rows) * cap, (a // a_rows + 1) * cap)
            fbr_ref[rows, lanes] = fb_ref[t, a]
            for_ref[rows, lanes] = fo_ref[t, a]
    w = w_ref[...].astype(BF16).astype(F32)
    for b in range(blocks):
        column = w[:, b : b + 1]
        for t in range(slots):
            e = ens_ref[t, :, b * BLOCK : (b + 1) * BLOCK].astype(F32)
            field[t, b : b + 1, :] = jnp.sum(e * column, axis=0, keepdims=True)
    for t in range(slots):
        f = field[t] * scale
        upper = f.astype(BF16)
        split[t, :blocks, :] = upper
        split[t, blocks:, :] = (f - upper.astype(F32)).astype(BF16)
    off_iota = lax.broadcasted_iota(jnp.int32, (BLOCK, 128), 0)
    blk_iota = lax.broadcasted_iota(jnp.int32, (blocks, 128), 0)
    per_slot = a_rows * groups

    @pl.loop(0, slots * a_rows)
    def _(step):
        base = pl.multiple_of(step * 8, 8)
        off = for_ref[pl.ds(base, 8), :]
        blk = fbr_ref[pl.ds(base, 8), :]
        hot = jnp.concatenate(
            [(off_iota == off[r : r + 1]).astype(F32).astype(BF16) for r in range(8)], axis=1
        )
        lhs = split[step // a_rows]
        proj = jnp.dot(lhs, hot, preferred_element_type=F32)
        value = proj[:blocks] + proj[blocks:]
        picked = [
            jnp.sum(
                jnp.where(blk_iota == blk[r : r + 1], value[:, r * 128 : (r + 1) * 128], 0.0),
                axis=0,
                keepdims=True,
            )
            for r in range(8)
        ]
        pick_ref[pl.ds(base, 8), :] = jnp.concatenate(picked, axis=0)


def join_kernel(pick_ref, owned_ref, out_ref):
    rows = pick_ref.shape[0]
    for peer in range(out_ref.shape[0]):
        out_ref[peer, :rows, :] = pick_ref[...]
        out_ref[peer, rows:, :] = owned_ref[...]


def gradient_kernel(ens_ref, got_ref, fbr_ref, for_ref, out_ref, res):
    slots, members, cells = ens_ref.shape
    blocks = cells // BLOCK
    groups = got_ref.shape[0]
    rows = fbr_ref.shape[0]
    tiles = got_ref.shape[1] - rows
    a_rows = rows // (slots * groups)
    quarters = tiles // a_rows
    cap = 128 // quarters
    quarter = lax.broadcasted_iota(jnp.int32, (groups, 128), 1) // cap

    def aligned(message, source, target):
        shift = (target - source) * cap % 128
        return pltpu.roll(message, shift, 1) if shift else message

    for a in range(a_rows):
        messages = [got_ref[:, rows + a + q * a_rows, :] for q in range(quarters)]
        for t in range(slots):
            w = jnp.zeros((groups, 128), F32)
            d = jnp.zeros((groups, 128), F32)
            for q in range(quarters):
                w = jnp.where(quarter == q, aligned(messages[q], t, q), w)
                d = jnp.where(quarter == q, aligned(messages[q], slots + t, q), d)
            at = pl.ds((t * a_rows + a) * groups, groups)
            x = got_ref[0, at, :]
            for peer in range(1, groups):
                x = x + got_ref[peer, at, :]
            res[at, :] = w * x - d
    off_iota = lax.broadcasted_iota(jnp.int32, (BLOCK, 128), 0)
    blk_iota = lax.broadcasted_iota(jnp.int32, (blocks, 128), 0)
    local = None
    for t in range(slots):

        def add_rows(step, total, t=t):
            base = pl.multiple_of((t * a_rows + step) * 8, 8)
            off = for_ref[pl.ds(base, 8), :]
            blk = fbr_ref[pl.ds(base, 8), :]
            value = res[pl.ds(base, 8), :]
            hot = jnp.concatenate(
                [(off_iota == off[r : r + 1]).astype(F32).astype(BF16) for r in range(8)], axis=1
            )
            placed = jnp.concatenate(
                [jnp.where(blk_iota == blk[r : r + 1], value[r : r + 1], 0.0) for r in range(8)],
                axis=1,
            )
            upper = placed.astype(BF16)
            lower = (placed - upper.astype(F32)).astype(BF16)
            both = jnp.concatenate([upper, lower], axis=0)
            return total + lax.dot_general(both, hot, NT, preferred_element_type=F32)

        total = lax.fori_loop(0, a_rows, add_rows, jnp.zeros((2 * blocks, BLOCK), F32))
        adjoint = (total[:blocks] + total[blocks:]).astype(BF16)
        lhs = jnp.concatenate(
            [ens_ref[t, :, b * BLOCK : (b + 1) * BLOCK] for b in range(blocks)], axis=0
        )
        prod = lax.dot_general(lhs, adjoint, NT, preferred_element_type=F32)
        part = prod.reshape(blocks, members, blocks)
        own = lax.broadcasted_iota(jnp.int32, part.shape, 0) == lax.broadcasted_iota(
            jnp.int32, part.shape, 2
        )
        part = jnp.sum(jnp.where(own, part, 0.0), axis=0)
        local = part if local is None else local + part
    padded = jnp.concatenate([local, jnp.zeros((members, 128 - blocks), F32)], axis=1)
    for peer in range(out_ref.shape[0]):
        out_ref[peer] = padded


def finish_kernel(scale, got_ref, w_ref, out_ref):
    total = got_ref[0]
    for peer in range(1, got_ref.shape[0]):
        total = total + got_ref[peer]
    out_ref[...] = w_ref[...] + scale * total[:, : w_ref.shape[1]]


def cost(flops, read):
    return pl.CostEstimate(flops=flops, bytes_accessed=read, transcendentals=0)


def shards(ens_pert, weights, foot_block, foot_offset, innovation, inv_var, obs_count):
    groups = lax.axis_size("member")
    windows = lax.axis_size("tm")
    slots, members, cells = ens_pert.shape
    blocks = cells // BLOCK
    tiles, _, cap = foot_block.shape[2:]
    rows = slots * tiles * groups * cap // 128
    scale = 1.0 / math.sqrt(members * groups - 1)
    foot_block = foot_block.reshape(slots, tiles, groups, cap)
    foot_offset = foot_offset.reshape(slots, tiles, groups, cap)
    owned = pl.pallas_call(
        owned_kernel,
        out_shape=jax.ShapeDtypeStruct((tiles, 128), F32),
        in_specs=[VMEM] * 3,
        out_specs=VMEM,
        compiler_params=PARAMS,
    )(
        innovation.reshape(slots, tiles, cap),
        inv_var.reshape(slots, tiles, cap),
        obs_count.reshape(slots, tiles),
    )
    owned = lax.all_to_all(owned, "space", 0, 0, tiled=True)
    pairs = 2 * blocks * rows * 128 * BLOCK
    picks, fbr, offr = pl.pallas_call(
        lambda *refs: pick_kernel(scale, *refs),
        out_shape=(
            jax.ShapeDtypeStruct((rows, 128), F32),
            jax.ShapeDtypeStruct((rows, 128), jnp.int32),
            jax.ShapeDtypeStruct((rows, 128), jnp.int32),
        ),
        in_specs=[VMEM] * 4,
        out_specs=(VMEM,) * 3,
        scratch_shapes=[
            pltpu.VMEM((slots, blocks, BLOCK), F32),
            pltpu.VMEM((slots, 2 * blocks, BLOCK), BF16),
        ],
        compiler_params=PARAMS,
        cost_estimate=cost(2 * pairs, 2 << 20),
    )(ens_pert, weights, foot_block, foot_offset)
    joined = pl.pallas_call(
        join_kernel,
        out_shape=jax.ShapeDtypeStruct((groups, rows + tiles, 128), F32),
        in_specs=[VMEM] * 2,
        out_specs=VMEM,
        compiler_params=PARAMS,
    )(picks, owned)
    got = lax.all_to_all(joined, "member", 0, 0, tiled=True)
    local = pl.pallas_call(
        gradient_kernel,
        out_shape=jax.ShapeDtypeStruct((windows, members, 128), F32),
        in_specs=[VMEM] * 4,
        out_specs=VMEM,
        scratch_shapes=[pltpu.VMEM((rows, 128), F32)],
        compiler_params=PARAMS,
    )(ens_pert, got, fbr, offr)
    parts = lax.all_to_all(local, "tm", 0, 0, tiled=True)
    return pl.pallas_call(
        lambda *refs: finish_kernel(scale, *refs),
        out_shape=jax.ShapeDtypeStruct(weights.shape, F32),
        in_specs=[VMEM] * 2,
        out_specs=VMEM,
        compiler_params=PARAMS,
    )(parts, weights)


def solution(mesh):
    in_specs = (
        P("tm", "member", "space"),
        P("member", "space"),
        P("tm", "space", None, None, None),
        P("tm", "space", None, None, None),
        P("tm", "space", "member", None, None),
        P("tm", "space", "member", None, None),
        P("tm", "space", "member", None),
    )
    out_specs = P("member", "space")
    return jax.shard_map(shards, mesh=mesh, in_specs=in_specs, out_specs=out_specs, check_vma=False)
```

```python
import math

import jax
import jax.numpy as jnp
from jax import lax
from jax.experimental import pallas as pl
from jax.experimental.pallas import tpu as pltpu
from jax.sharding import PartitionSpec as P

BLOCK = 256
VMEM = pl.BlockSpec(memory_space=pltpu.VMEM)
HBM = pl.BlockSpec(memory_space=pltpu.HBM)
PARAMS = pltpu.CompilerParams(vmem_limit_bytes=32 * 1024 * 1024)
F32, BF16 = jnp.float32, jnp.bfloat16
NT = (((1,), (1,)), ((), ()))


def owned_kernel(
    innov_hbm, var_hbm, count_hbm, fb_hbm, fo_hbm, w_hbm, ens_hbm,
    out_ref, fb_ref, fo_ref, w_ref, ens_ref, innov_ref, var_ref, count_ref, sems,
):
    pairs = (
        (count_hbm, count_ref),
        (var_hbm, var_ref),
        (innov_hbm, innov_ref),
        (fo_hbm, fo_ref),
        (fb_hbm, fb_ref),
        (w_hbm, w_ref),
        (ens_hbm, ens_ref),
    )
    copies = [pltpu.make_async_copy(src, dst, sems.at[i]) for i, (src, dst) in enumerate(pairs)]
    for copy in copies:
        copy.start()
    slots, tiles, cap = innov_ref.shape
    diag = lax.broadcasted_iota(jnp.int32, (tiles, tiles), 0) == lax.broadcasted_iota(
        jnp.int32, (tiles, tiles), 1
    )
    lane = lax.broadcasted_iota(jnp.int32, (tiles, cap), 1).astype(F32)
    copies[0].wait()
    columns = []
    for t in range(slots):
        row = count_ref[t : t + 1, :].astype(F32)
        columns.append(jnp.sum(jnp.where(diag, row, 0.0), axis=1, keepdims=True))
    copies[1].wait()
    copies[2].wait()
    out_ref[...] = jnp.concatenate(
        [jnp.where(lane < columns[t], var_ref[t], 0.0) for t in range(slots)]
        + [innov_ref[t] for t in range(slots)],
        axis=1,
    )
    for copy in copies[3:]:
        copy.wait()


def pick_kernel(scale, ens_ref, w_ref, fb_ref, fo_ref, pick_ref, offr, mask_ref, fbr, field, split):
    slots, members, cells = ens_ref.shape
    blocks = cells // BLOCK
    tiles, groups, cap = fb_ref.shape[1:]
    quarters = 128 // cap
    a_rows = tiles // quarters
    for t in range(slots):
        for a in range(tiles):
            rows = pl.ds((t * a_rows + a % a_rows) * groups, groups)
            lanes = slice((a // a_rows) * cap, (a // a_rows + 1) * cap)
            fbr[rows, lanes] = fb_ref[t, a]
            offr[rows, lanes] = fo_ref[t, a]
    w = w_ref[...].astype(BF16).astype(F32)
    for b in range(blocks):
        column = w[:, b : b + 1]
        for t in range(slots):
            e = ens_ref[t, :, b * BLOCK : (b + 1) * BLOCK].astype(F32)
            field[t, b : b + 1, :] = jnp.sum(e * column, axis=0, keepdims=True)
    for t in range(slots):
        f = field[t] * scale
        upper = f.astype(BF16)
        split[t, :blocks, :] = upper
        split[t, blocks:, :] = (f - upper.astype(F32)).astype(BF16)
    off_iota = lax.broadcasted_iota(jnp.int32, (BLOCK, 128), 0)
    blk_iota = lax.broadcasted_iota(jnp.int32, (blocks, 128), 0)

    @pl.loop(0, slots * a_rows)
    def _(step):
        base = pl.multiple_of(step * groups, groups)
        off = offr[pl.ds(base, groups), :]
        blk = fbr[pl.ds(base, groups), :]
        lhs = split[step // a_rows]
        hot = jnp.concatenate(
            [(off_iota == off[r : r + 1]).astype(F32).astype(BF16) for r in range(groups)], axis=1
        )
        proj = jnp.dot(lhs, hot, preferred_element_type=F32)
        value = proj[:blocks] + proj[blocks:]
        own = jnp.concatenate(
            [(blk_iota == blk[r : r + 1]).astype(F32) for r in range(groups)], axis=1
        )
        mask_ref[step] = own.astype(BF16)
        picked = jnp.sum(own * value, axis=0, keepdims=True)
        pick_ref[pl.ds(base, groups), :] = jnp.concatenate(
            [picked[:, r * 128 : (r + 1) * 128] for r in range(groups)], axis=0
        )


def join_kernel(pick_ref, owned_ref, out_ref):
    rows = pick_ref.shape[0]
    for peer in range(out_ref.shape[0]):
        out_ref[peer, :rows, :] = pick_ref[...]
        out_ref[peer, rows:, :] = owned_ref[...]


def gradient_kernel(ens_ref, got_ref, off_ref, mask_ref, out_ref, res):
    slots, members, cells = ens_ref.shape
    blocks = cells // BLOCK
    groups = got_ref.shape[0]
    a_rows = mask_ref.shape[0] // slots
    rows = slots * a_rows * groups
    tiles = got_ref.shape[1] - rows
    quarters = tiles // a_rows
    cap = 128 // quarters
    quarter = lax.broadcasted_iota(jnp.int32, (groups, 128), 1) // cap

    def aligned(message, source, target):
        shift = (target - source) * cap % 128
        return pltpu.roll(message, shift, 1) if shift else message

    for a in range(a_rows):
        messages = [got_ref[:, rows + a + q * a_rows, :] for q in range(quarters)]
        for t in range(slots):
            w = jnp.zeros((groups, 128), F32)
            i = jnp.zeros((groups, 128), F32)
            for q in range(quarters):
                w = jnp.where(quarter == q, aligned(messages[q], t, q), w)
                i = jnp.where(quarter == q, aligned(messages[q], slots + t, q), i)
            at = pl.ds((t * a_rows + a) * groups, groups)
            x = got_ref[0, at, :]
            for peer in range(1, groups):
                x = x + got_ref[peer, at, :]
            res[at, :] = w * (x - i)
    off_iota = lax.broadcasted_iota(jnp.int32, (BLOCK, 128), 0)
    local = None
    for t in range(slots):
        total = jnp.zeros((2 * blocks, BLOCK), F32)
        for step in range(t * a_rows, (t + 1) * a_rows):
            value = res[step * groups : (step + 1) * groups, :]
            upper = value.astype(BF16)
            lower = (value - upper.astype(F32)).astype(BF16)
            own = mask_ref[step]
            both = jnp.concatenate(
                [
                    jnp.concatenate(
                        [own[:, r * 128 : (r + 1) * 128] * part[r : r + 1] for r in range(groups)],
                        axis=1,
                    )
                    for part in (upper, lower)
                ],
                axis=0,
            )
            off = off_ref[step * groups : (step + 1) * groups, :]
            hot = jnp.concatenate(
                [(off_iota == off[r : r + 1]).astype(F32).astype(BF16) for r in range(groups)],
                axis=1,
            )
            total += lax.dot_general(both, hot, NT, preferred_element_type=F32)
        adjoint = (total[:blocks] + total[blocks:]).astype(BF16)
        lhs = jnp.concatenate(
            [ens_ref[t, :, b * BLOCK : (b + 1) * BLOCK] for b in range(blocks)], axis=0
        )
        prod = lax.dot_general(lhs, adjoint, NT, preferred_element_type=F32)
        part = prod.reshape(blocks, members, blocks)
        own = lax.broadcasted_iota(jnp.int32, part.shape, 0) == lax.broadcasted_iota(
            jnp.int32, part.shape, 2
        )
        part = jnp.sum(jnp.where(own, part, 0.0), axis=0)
        local = part if local is None else local + part
    padded = jnp.concatenate([local, jnp.zeros((members, 128 - blocks), F32)], axis=1)
    for peer in range(out_ref.shape[0]):
        out_ref[peer] = padded


def finish_kernel(scale, got_ref, w_ref, out_ref):
    total = got_ref[0]
    for peer in range(1, got_ref.shape[0]):
        total = total + got_ref[peer]
    out_ref[...] = w_ref[...] + scale * total[:, : w_ref.shape[1]]


def cost(flops, read):
    return pl.CostEstimate(flops=flops, bytes_accessed=read, transcendentals=0)


def in_hbm(array):
    return pltpu.with_memory_space_constraint(array, pltpu.HBM)


def in_vmem(shape, dtype):
    return pltpu.VMEM(shape, dtype)


def shards(ens_pert, weights, foot_block, foot_offset, innovation, inv_var, obs_count):
    groups = lax.axis_size("member")
    windows = lax.axis_size("tm")
    slots, members, cells = ens_pert.shape
    blocks = cells // BLOCK
    tiles, _, cap = foot_block.shape[2:]
    rows = slots * tiles * groups * cap // 128
    steps = rows // groups
    scale = 1.0 / math.sqrt(members * groups - 1)
    owned, fb, fo, w, ens = pl.pallas_call(
        owned_kernel,
        out_shape=(
            jax.ShapeDtypeStruct((tiles, 128), F32),
            in_vmem((slots, tiles, groups, cap), jnp.int32),
            in_vmem((slots, tiles, groups, cap), jnp.int32),
            in_vmem(weights.shape, F32),
            in_vmem(ens_pert.shape, BF16),
        ),
        in_specs=[HBM] * 7,
        out_specs=(VMEM,) * 5,
        scratch_shapes=[
            pltpu.VMEM((slots, tiles, cap), F32),
            pltpu.VMEM((slots, tiles, cap), F32),
            pltpu.VMEM((slots, tiles), jnp.int32),
            pltpu.SemaphoreType.DMA((7,)),
        ],
        compiler_params=PARAMS,
    )(
        in_hbm(innovation.reshape(slots, tiles, cap)),
        in_hbm(inv_var.reshape(slots, tiles, cap)),
        in_hbm(obs_count.reshape(slots, tiles)),
        in_hbm(foot_block.reshape(slots, tiles, groups, cap)),
        in_hbm(foot_offset.reshape(slots, tiles, groups, cap)),
        in_hbm(weights),
        in_hbm(ens_pert),
    )
    owned = lax.all_to_all(owned, "space", 0, 0, tiled=True)
    picks, offsets, mask = pl.pallas_call(
        lambda *refs: pick_kernel(scale, *refs),
        out_shape=(
            in_vmem((rows, 128), F32),
            in_vmem((rows, 128), jnp.int32),
            in_vmem((steps, blocks, groups * 128), BF16),
        ),
        in_specs=[VMEM] * 4,
        out_specs=(VMEM,) * 3,
        scratch_shapes=[
            pltpu.VMEM((rows, 128), jnp.int32),
            pltpu.VMEM((slots, blocks, BLOCK), F32),
            pltpu.VMEM((slots, 2 * blocks, BLOCK), BF16),
        ],
        compiler_params=PARAMS,
        cost_estimate=cost(4 * blocks * rows * 128 * BLOCK, 2 << 20),
    )(ens, w, fb, fo)
    joined = pl.pallas_call(
        join_kernel,
        out_shape=jax.ShapeDtypeStruct((groups, rows + tiles, 128), F32),
        in_specs=[VMEM] * 2,
        out_specs=VMEM,
        compiler_params=PARAMS,
    )(picks, owned)
    got = lax.all_to_all(joined, "member", 0, 0, tiled=True)
    local = pl.pallas_call(
        gradient_kernel,
        out_shape=jax.ShapeDtypeStruct((windows, members, 128), F32),
        in_specs=[VMEM] * 4,
        out_specs=VMEM,
        scratch_shapes=[pltpu.VMEM((rows, 128), F32)],
        compiler_params=PARAMS,
    )(ens, got, offsets, mask)
    parts = lax.all_to_all(local, "tm", 0, 0, tiled=True)
    return pl.pallas_call(
        lambda *refs: finish_kernel(scale, *refs),
        out_shape=jax.ShapeDtypeStruct(weights.shape, F32),
        in_specs=[VMEM] * 2,
        out_specs=VMEM,
        compiler_params=PARAMS,
    )(parts, w)


def solution(mesh):
    in_specs = (
        P("tm", "member", "space"),
        P("member", "space"),
        P("tm", "space", None, None, None),
        P("tm", "space", None, None, None),
        P("tm", "space", "member", None, None),
        P("tm", "space", "member", None, None),
        P("tm", "space", "member", None),
    )
    out_specs = P("member", "space")
    return jax.shard_map(shards, mesh=mesh, in_specs=in_specs, out_specs=out_specs, check_vma=False)
```

```python
import math

import jax
import jax.numpy as jnp
from jax import lax
from jax.experimental import pallas as pl
from jax.experimental.pallas import tpu as pltpu
from jax.sharding import PartitionSpec as P

BLOCK = 256
LANES = 128
VMEM = pl.BlockSpec(memory_space=pltpu.VMEM)
HBM = pl.BlockSpec(memory_space=pltpu.HBM)
PARAMS = pltpu.CompilerParams(vmem_limit_bytes=32 * 1024 * 1024)
F32, BF16 = jnp.float32, jnp.bfloat16
NT = (((1,), (1,)), ((), ()))


def fetch(sems, *pairs):
    copies = [pltpu.make_async_copy(src, dst, sems.at[i]) for i, (src, dst) in enumerate(pairs)]
    for copy in copies:
        copy.start()
    return copies


def owned_kernel(innov_hbm, var_hbm, count_hbm, out_ref, innov_ref, var_ref, count_ref, sems):
    copies = fetch(sems, (count_hbm, count_ref), (var_hbm, var_ref), (innov_hbm, innov_ref))
    slots, tiles, cap = innov_ref.shape
    diag = lax.broadcasted_iota(jnp.int32, (tiles, tiles), 0) == lax.broadcasted_iota(
        jnp.int32, (tiles, tiles), 1
    )
    lane = lax.broadcasted_iota(jnp.int32, (tiles, cap), 1).astype(F32)
    copies[0].wait()
    columns = []
    for t in range(slots):
        row = count_ref[t : t + 1, :].astype(F32)
        columns.append(jnp.sum(jnp.where(diag, row, 0.0), axis=1, keepdims=True))
    copies[1].wait()
    copies[2].wait()
    out_ref[...] = jnp.concatenate(
        [jnp.where(lane < columns[t], var_ref[t], 0.0) for t in range(slots)]
        + [innov_ref[t] for t in range(slots)],
        axis=1,
    )


def hot_rows(ids, count):
    iota = lax.broadcasted_iota(jnp.int32, (count, LANES), 0)
    return jnp.concatenate(
        [(iota == ids[r : r + 1]).astype(F32) for r in range(ids.shape[0])], axis=1
    )


def pick_kernel(
    scale, ens_hbm, w_hbm, fb_hbm, fo_hbm, pick_ref, hot_ref, high_ref,
    ens_ref, w_ref, fb_ref, fo_ref, low, field, split, sems,
):
    copies = fetch(sems, (fo_hbm, fo_ref), (fb_hbm, fb_ref), (w_hbm, w_ref), (ens_hbm, ens_ref))
    slots, members, cells = ens_ref.shape
    blocks = cells // BLOCK
    highs = cells // LANES
    tiles, groups, cap = fb_ref.shape[1:]
    quarters = LANES // cap
    a_rows = tiles // quarters
    copies[0].wait()
    copies[1].wait()
    for t in range(slots):
        for a in range(tiles):
            rows = pl.ds((t * a_rows + a % a_rows) * groups, groups)
            lanes = slice((a // a_rows) * cap, (a // a_rows + 1) * cap)
            offset = fo_ref[t, a]
            upper_half = offset >= LANES
            high_ref[rows, lanes] = fb_ref[t, a] + jnp.where(upper_half, blocks, 0)
            low[rows, lanes] = jnp.where(upper_half, offset - LANES, offset)
    copies[2].wait()
    copies[3].wait()
    w = w_ref[...].astype(BF16).astype(F32)
    for b in range(blocks):
        column = w[:, b : b + 1]
        for t in range(slots):
            e = ens_ref[t, :, b * BLOCK : (b + 1) * BLOCK].astype(F32)
            sums = jnp.sum(e * column, axis=0, keepdims=True)
            field[t, b : b + 1, :] = sums[:, :LANES]
            field[t, blocks + b : blocks + b + 1, :] = sums[:, LANES:]
    for t in range(slots):
        f = field[t] * scale
        upper = f.astype(BF16)
        split[t, :highs, :] = upper
        split[t, highs:, :] = (f - upper.astype(F32)).astype(BF16)

    @pl.loop(0, slots * a_rows)
    def _(step):
        base = pl.multiple_of(step * groups, groups)
        hot = hot_rows(low[pl.ds(base, groups), :], LANES).astype(BF16)
        hot_ref[step] = hot.T
        proj = jnp.dot(split[step // a_rows], hot, preferred_element_type=F32)
        own = hot_rows(high_ref[pl.ds(base, groups), :], highs)
        picked = jnp.sum(own * (proj[:highs] + proj[highs:]), axis=0, keepdims=True)
        pick_ref[pl.ds(base, groups), :] = jnp.concatenate(
            [picked[:, r * LANES : (r + 1) * LANES] for r in range(groups)], axis=0
        )


def join_kernel(pick_ref, owned_ref, out_ref):
    groups = out_ref.shape[0]
    rows = pick_ref.shape[0]
    tiles = owned_ref.shape[0]
    a_rows = (out_ref.shape[1] - rows) // 2
    quarters = tiles // a_rows
    cap = LANES // quarters
    slots = rows // (a_rows * groups)
    quarter = lax.broadcasted_iota(jnp.int32, (a_rows, LANES), 1) // cap
    sublane = lax.broadcasted_iota(jnp.int32, (groups, LANES), 0)
    own_group = sublane == lax.axis_index("member")

    def aligned(source):
        total = None
        for q in range(quarters):
            part = owned_ref[q * a_rows : (q + 1) * a_rows, :]
            shift = (q - source) * cap % LANES
            part = pltpu.roll(part, shift, 1) if shift else part
            total = part if total is None else jnp.where(quarter == q, part, total)
        return total

    weights = jnp.concatenate([aligned(t) for t in range(slots)], axis=0)
    for t in range(slots):
        innov = aligned(slots + t)
        for a in range(a_rows):
            at = slice((t * a_rows + a) * groups, (t * a_rows + a + 1) * groups)
            value = pick_ref[at, :] - jnp.where(own_group, innov[a : a + 1], 0.0)
            for peer in range(groups):
                out_ref[peer, at, :] = value
    for peer in range(groups):
        out_ref[peer, rows:, :] = weights


def gradient_kernel(ens_ref, got_ref, hot_ref, high_ref, out_ref):
    slots, members, cells = ens_ref.shape
    blocks = cells // BLOCK
    highs = cells // LANES
    groups = got_ref.shape[0]
    rows = high_ref.shape[0]
    a_rows = rows // (slots * groups)
    local = None
    for t in range(slots):
        total = jnp.zeros((2 * highs, LANES), F32)
        for step in range(t * a_rows, (t + 1) * a_rows):
            at = slice(step * groups, (step + 1) * groups)
            value = got_ref[0, at, :]
            for peer in range(1, groups):
                value = value + got_ref[peer, at, :]
            value = value * got_ref[:, rows + step, :]
            upper = value.astype(BF16)
            lower = (value - upper.astype(F32)).astype(BF16)
            own = hot_rows(high_ref[at, :], highs).astype(BF16)
            both = jnp.concatenate(
                [
                    jnp.concatenate(
                        [
                            own[:, r * LANES : (r + 1) * LANES] * part[r : r + 1]
                            for r in range(groups)
                        ],
                        axis=1,
                    )
                    for part in (upper, lower)
                ],
                axis=0,
            )
            total += jnp.dot(both, hot_ref[step], preferred_element_type=F32)
        adjoint = (total[:highs] + total[highs:]).astype(BF16)
        adjoint = jnp.concatenate([adjoint[:blocks], adjoint[blocks:]], axis=1)
        lhs = jnp.concatenate(
            [ens_ref[t, :, b * BLOCK : (b + 1) * BLOCK] for b in range(blocks)], axis=0
        )
        prod = lax.dot_general(lhs, adjoint, NT, preferred_element_type=F32)
        part = prod.reshape(blocks, members, blocks)
        own = lax.broadcasted_iota(jnp.int32, part.shape, 0) == lax.broadcasted_iota(
            jnp.int32, part.shape, 2
        )
        part = jnp.sum(jnp.where(own, part, 0.0), axis=0)
        local = part if local is None else local + part
    height = out_ref.shape[1]
    dense = jnp.concatenate(
        [local[r : r + height] for r in range(0, members, height)], axis=1
    )
    for peer in range(out_ref.shape[0]):
        out_ref[peer] = dense


def finish_kernel(scale, got_ref, w_ref, out_ref):
    total = got_ref[0]
    for peer in range(1, got_ref.shape[0]):
        total = total + got_ref[peer]
    blocks = w_ref.shape[1]
    total = jnp.concatenate(
        [total[:, c : c + blocks] for c in range(0, LANES, blocks)], axis=0
    )
    out_ref[...] = w_ref[...] + scale * total


def cost(flops, read):
    return pl.CostEstimate(flops=flops, bytes_accessed=read, transcendentals=0)


def in_hbm(array):
    return pltpu.with_memory_space_constraint(array, pltpu.HBM)


def in_vmem(shape, dtype):
    return pltpu.VMEM(shape, dtype)


def shards(ens_pert, weights, foot_block, foot_offset, innovation, inv_var, obs_count):
    groups = lax.axis_size("member")
    windows = lax.axis_size("tm")
    slots, members, cells = ens_pert.shape
    blocks = cells // BLOCK
    highs = cells // LANES
    tiles, _, cap = foot_block.shape[2:]
    rows = slots * tiles * groups * cap // LANES
    steps = rows // groups
    scale = 1.0 / math.sqrt(members * groups - 1)
    owned = pl.pallas_call(
        owned_kernel,
        out_shape=jax.ShapeDtypeStruct((tiles, LANES), F32),
        in_specs=[HBM] * 3,
        out_specs=VMEM,
        scratch_shapes=[
            pltpu.VMEM((slots, tiles, cap), F32),
            pltpu.VMEM((slots, tiles, cap), F32),
            pltpu.VMEM((slots, tiles), jnp.int32),
            pltpu.SemaphoreType.DMA((3,)),
        ],
        compiler_params=PARAMS,
    )(
        in_hbm(innovation.reshape(slots, tiles, cap)),
        in_hbm(inv_var.reshape(slots, tiles, cap)),
        in_hbm(obs_count.reshape(slots, tiles)),
    )
    owned = lax.all_to_all(owned, "space", 0, 0, tiled=True)
    picks, hot, high = pl.pallas_call(
        lambda *refs: pick_kernel(scale, *refs),
        out_shape=(
            in_vmem((rows, LANES), F32),
            in_vmem((steps, groups * LANES, LANES), BF16),
            in_vmem((rows, LANES), jnp.int32),
        ),
        in_specs=[HBM] * 4,
        out_specs=(VMEM,) * 3,
        scratch_shapes=[
            pltpu.VMEM(ens_pert.shape, BF16),
            pltpu.VMEM(weights.shape, F32),
            pltpu.VMEM((slots, tiles, groups, cap), jnp.int32),
            pltpu.VMEM((slots, tiles, groups, cap), jnp.int32),
            pltpu.VMEM((rows, LANES), jnp.int32),
            pltpu.VMEM((slots, highs, LANES), F32),
            pltpu.VMEM((slots, 2 * highs, LANES), BF16),
            pltpu.SemaphoreType.DMA((4,)),
        ],
        compiler_params=PARAMS,
        cost_estimate=cost(4 * blocks * rows * LANES * BLOCK, 4 << 20),
    )(
        in_hbm(ens_pert),
        in_hbm(weights),
        in_hbm(foot_block.reshape(slots, tiles, groups, cap)),
        in_hbm(foot_offset.reshape(slots, tiles, groups, cap)),
    )
    joined = pl.pallas_call(
        join_kernel,
        out_shape=jax.ShapeDtypeStruct((groups, rows + steps, LANES), F32),
        in_specs=[VMEM] * 2,
        out_specs=VMEM,
        compiler_params=PARAMS,
    )(picks, owned)
    got = lax.all_to_all(joined, "member", 0, 0, tiled=True)
    local = pl.pallas_call(
        gradient_kernel,
        out_shape=jax.ShapeDtypeStruct((windows, members * blocks // LANES, LANES), F32),
        in_specs=[VMEM] * 4,
        out_specs=VMEM,
        compiler_params=PARAMS,
    )(ens_pert, got, hot, high)
    parts = lax.all_to_all(local, "tm", 0, 0, tiled=True)
    return pl.pallas_call(
        lambda *refs: finish_kernel(scale, *refs),
        out_shape=jax.ShapeDtypeStruct(weights.shape, F32),
        in_specs=[VMEM] * 2,
        out_specs=VMEM,
        compiler_params=PARAMS,
    )(parts, weights)


def solution(mesh):
    in_specs = (
        P("tm", "member", "space"),
        P("member", "space"),
        P("tm", "space", None, None, None),
        P("tm", "space", None, None, None),
        P("tm", "space", "member", None, None),
        P("tm", "space", "member", None, None),
        P("tm", "space", "member", None),
    )
    out_specs = P("member", "space")
    return jax.shard_map(shards, mesh=mesh, in_specs=in_specs, out_specs=out_specs, check_vma=False)
```

```python
import math

import jax
import jax.numpy as jnp
from jax import lax
from jax.experimental import pallas as pl
from jax.experimental.pallas import tpu as pltpu
from jax.sharding import PartitionSpec as P

BLOCK = 256
LANES = 128
VMEM = pl.BlockSpec(memory_space=pltpu.VMEM)
HBM = pl.BlockSpec(memory_space=pltpu.HBM)
PARAMS = pltpu.CompilerParams(vmem_limit_bytes=32 * 1024 * 1024)
F32, BF16 = jnp.float32, jnp.bfloat16


def fetch(sems, *pairs):
    copies = [pltpu.make_async_copy(src, dst, sems.at[i]) for i, (src, dst) in enumerate(pairs)]
    for copy in copies:
        copy.start()
    return copies


def owned_kernel(innov_hbm, var_hbm, count_hbm, out_ref, innov_ref, var_ref, count_ref, sems):
    copies = fetch(sems, (count_hbm, count_ref), (var_hbm, var_ref), (innov_hbm, innov_ref))
    slots, tiles, cap = innov_ref.shape
    diag = lax.broadcasted_iota(jnp.int32, (tiles, tiles), 0) == lax.broadcasted_iota(
        jnp.int32, (tiles, tiles), 1
    )
    lane = lax.broadcasted_iota(jnp.int32, (tiles, cap), 1).astype(F32)
    copies[0].wait()
    columns = []
    for t in range(slots):
        row = count_ref[t : t + 1, :].astype(F32)
        columns.append(jnp.sum(jnp.where(diag, row, 0.0), axis=1, keepdims=True))
    copies[1].wait()
    copies[2].wait()
    out_ref[...] = jnp.concatenate(
        [jnp.where(lane < columns[t], var_ref[t], 0.0) for t in range(slots)]
        + [innov_ref[t] for t in range(slots)],
        axis=1,
    )


def hot_rows(ids, count):
    iota = lax.broadcasted_iota(jnp.int32, (count, LANES), 0)
    return jnp.concatenate(
        [(iota == ids[r : r + 1]).astype(F32) for r in range(ids.shape[0])], axis=1
    )


def pick_kernel(
    scale, ens_hbm, w_hbm, fb_hbm, fo_hbm, pick_ref, hot_ref, high_ref,
    ens_ref, w_ref, fb_ref, fo_ref, low, field, split, sems,
):
    copies = fetch(sems, (fo_hbm, fo_ref), (fb_hbm, fb_ref), (w_hbm, w_ref), (ens_hbm, ens_ref))
    slots, members, cells = ens_ref.shape
    blocks = cells // BLOCK
    highs = cells // LANES
    tiles, groups, cap = fb_ref.shape[1:]
    quarters = LANES // cap
    a_rows = tiles // quarters
    copies[0].wait()
    copies[1].wait()
    for t in range(slots):
        for a in range(tiles):
            rows = pl.ds((t * a_rows + a % a_rows) * groups, groups)
            lanes = slice((a // a_rows) * cap, (a // a_rows + 1) * cap)
            offset = fo_ref[t, a]
            upper_half = offset >= LANES
            high_ref[rows, lanes] = fb_ref[t, a] + jnp.where(upper_half, blocks, 0)
            low[rows, lanes] = jnp.where(upper_half, offset - LANES, offset)
    copies[2].wait()
    copies[3].wait()
    w = w_ref[...].astype(BF16).astype(F32)
    for b in range(blocks):
        column = w[:, b : b + 1]
        for t in range(slots):
            e = ens_ref[t, :, b * BLOCK : (b + 1) * BLOCK].astype(F32)
            sums = jnp.sum(e * column, axis=0, keepdims=True)
            field[t, b : b + 1, :] = sums[:, :LANES]
            field[t, blocks + b : blocks + b + 1, :] = sums[:, LANES:]
    for t in range(slots):
        f = field[t] * scale
        upper = f.astype(BF16)
        split[t, :highs, :] = upper
        split[t, highs:, :] = (f - upper.astype(F32)).astype(BF16)

    @pl.loop(0, slots * a_rows)
    def _(step):
        base = pl.multiple_of(step * groups, groups)
        hot = hot_rows(low[pl.ds(base, groups), :], LANES).astype(BF16)
        hot_ref[step] = hot.T
        proj = jnp.dot(split[step // a_rows], hot, preferred_element_type=F32)
        own = hot_rows(high_ref[pl.ds(base, groups), :], highs)
        picked = jnp.sum(own * (proj[:highs] + proj[highs:]), axis=0, keepdims=True)
        pick_ref[pl.ds(base, groups), :] = jnp.concatenate(
            [picked[:, r * LANES : (r + 1) * LANES] for r in range(groups)], axis=0
        )


def join_kernel(pick_ref, owned_ref, out_ref):
    groups = out_ref.shape[0]
    rows = pick_ref.shape[0]
    tiles = owned_ref.shape[0]
    a_rows = (out_ref.shape[1] - rows) // 2
    quarters = tiles // a_rows
    cap = LANES // quarters
    slots = rows // (a_rows * groups)
    quarter = lax.broadcasted_iota(jnp.int32, (a_rows, LANES), 1) // cap
    sublane = lax.broadcasted_iota(jnp.int32, (groups, LANES), 0)
    own_group = sublane == lax.axis_index("member")

    def aligned(source):
        total = None
        for q in range(quarters):
            part = owned_ref[q * a_rows : (q + 1) * a_rows, :]
            shift = (q - source) * cap % LANES
            part = pltpu.roll(part, shift, 1) if shift else part
            total = part if total is None else jnp.where(quarter == q, part, total)
        return total

    weights = jnp.concatenate([aligned(t) for t in range(slots)], axis=0)
    for t in range(slots):
        innov = aligned(slots + t)
        for a in range(a_rows):
            at = slice((t * a_rows + a) * groups, (t * a_rows + a + 1) * groups)
            value = pick_ref[at, :] - jnp.where(own_group, innov[a : a + 1], 0.0)
            for peer in range(groups):
                out_ref[peer, at, :] = value
    for peer in range(groups):
        out_ref[peer, rows:, :] = weights


def gradient_kernel(ens_ref, got_ref, hot_ref, high_ref, out_ref):
    slots, members, cells = ens_ref.shape
    blocks = cells // BLOCK
    highs = cells // LANES
    groups = got_ref.shape[0]
    rows = high_ref.shape[0]
    a_rows = rows // (slots * groups)
    sums = [None] * blocks
    for t in range(slots):
        total = jnp.zeros((2 * highs, LANES), F32)
        for step in range(t * a_rows, (t + 1) * a_rows):
            at = slice(step * groups, (step + 1) * groups)
            value = got_ref[0, at, :]
            for peer in range(1, groups):
                value = value + got_ref[peer, at, :]
            value = value * got_ref[:, rows + step, :]
            upper = value.astype(BF16)
            lower = (value - upper.astype(F32)).astype(BF16)
            own = hot_rows(high_ref[at, :], highs).astype(BF16)
            both = jnp.concatenate(
                [
                    jnp.concatenate(
                        [
                            own[:, r * LANES : (r + 1) * LANES] * part[r : r + 1]
                            for r in range(groups)
                        ],
                        axis=1,
                    )
                    for part in (upper, lower)
                ],
                axis=0,
            )
            total += jnp.dot(both, hot_ref[step], preferred_element_type=F32)
        adjoint = (total[:highs] + total[highs:]).astype(BF16)
        adjoint = jnp.concatenate([adjoint[:blocks], adjoint[blocks:]], axis=1)
        adjoint = adjoint.astype(F32)
        for b in range(blocks):
            e = ens_ref[t, :, b * BLOCK : (b + 1) * BLOCK].astype(F32) * adjoint[b : b + 1]
            e = e[:, :LANES] + e[:, LANES:]
            sums[b] = e if t == 0 else sums[b] + e
    local = jnp.concatenate([jnp.sum(e, axis=1, keepdims=True) for e in sums], axis=1)
    height = out_ref.shape[1]
    dense = jnp.concatenate(
        [local[r : r + height] for r in range(0, members, height)], axis=1
    )
    for peer in range(out_ref.shape[0]):
        out_ref[peer] = dense


def finish_kernel(scale, got_ref, w_ref, out_ref):
    total = got_ref[0]
    for peer in range(1, got_ref.shape[0]):
        total = total + got_ref[peer]
    blocks = w_ref.shape[1]
    total = jnp.concatenate(
        [total[:, c : c + blocks] for c in range(0, LANES, blocks)], axis=0
    )
    out_ref[...] = w_ref[...] + scale * total


def cost(flops, read):
    return pl.CostEstimate(flops=flops, bytes_accessed=read, transcendentals=0)


def in_hbm(array):
    return pltpu.with_memory_space_constraint(array, pltpu.HBM)


def in_vmem(shape, dtype):
    return pltpu.VMEM(shape, dtype)


def shards(ens_pert, weights, foot_block, foot_offset, innovation, inv_var, obs_count):
    groups = lax.axis_size("member")
    windows = lax.axis_size("tm")
    slots, members, cells = ens_pert.shape
    blocks = cells // BLOCK
    highs = cells // LANES
    tiles, _, cap = foot_block.shape[2:]
    rows = slots * tiles * groups * cap // LANES
    steps = rows // groups
    scale = 1.0 / math.sqrt(members * groups - 1)
    owned = pl.pallas_call(
        owned_kernel,
        out_shape=jax.ShapeDtypeStruct((tiles, LANES), F32),
        in_specs=[HBM] * 3,
        out_specs=VMEM,
        scratch_shapes=[
            pltpu.VMEM((slots, tiles, cap), F32),
            pltpu.VMEM((slots, tiles, cap), F32),
            pltpu.VMEM((slots, tiles), jnp.int32),
            pltpu.SemaphoreType.DMA((3,)),
        ],
        compiler_params=PARAMS,
    )(
        in_hbm(innovation.reshape(slots, tiles, cap)),
        in_hbm(inv_var.reshape(slots, tiles, cap)),
        in_hbm(obs_count.reshape(slots, tiles)),
    )
    owned = lax.all_to_all(owned, "space", 0, 0, tiled=True)
    picks, hot, high = pl.pallas_call(
        lambda *refs: pick_kernel(scale, *refs),
        out_shape=(
            in_vmem((rows, LANES), F32),
            in_vmem((steps, groups * LANES, LANES), BF16),
            in_vmem((rows, LANES), jnp.int32),
        ),
        in_specs=[HBM] * 4,
        out_specs=(VMEM,) * 3,
        scratch_shapes=[
            pltpu.VMEM(ens_pert.shape, BF16),
            pltpu.VMEM(weights.shape, F32),
            pltpu.VMEM((slots, tiles, groups, cap), jnp.int32),
            pltpu.VMEM((slots, tiles, groups, cap), jnp.int32),
            pltpu.VMEM((rows, LANES), jnp.int32),
            pltpu.VMEM((slots, highs, LANES), F32),
            pltpu.VMEM((slots, 2 * highs, LANES), BF16),
            pltpu.SemaphoreType.DMA((4,)),
        ],
        compiler_params=PARAMS,
        cost_estimate=cost(4 * blocks * rows * LANES * BLOCK, 4 << 20),
    )(
        in_hbm(ens_pert),
        in_hbm(weights),
        in_hbm(foot_block.reshape(slots, tiles, groups, cap)),
        in_hbm(foot_offset.reshape(slots, tiles, groups, cap)),
    )
    joined = pl.pallas_call(
        join_kernel,
        out_shape=jax.ShapeDtypeStruct((groups, rows + steps, LANES), F32),
        in_specs=[VMEM] * 2,
        out_specs=VMEM,
        compiler_params=PARAMS,
    )(picks, owned)
    got = lax.all_to_all(joined, "member", 0, 0, tiled=True)
    local = pl.pallas_call(
        gradient_kernel,
        out_shape=jax.ShapeDtypeStruct((windows, members * blocks // LANES, LANES), F32),
        in_specs=[VMEM] * 4,
        out_specs=VMEM,
        compiler_params=PARAMS,
    )(ens_pert, got, hot, high)
    parts = lax.all_to_all(local, "tm", 0, 0, tiled=True)
    return pl.pallas_call(
        lambda *refs: finish_kernel(scale, *refs),
        out_shape=jax.ShapeDtypeStruct(weights.shape, F32),
        in_specs=[VMEM] * 2,
        out_specs=VMEM,
        compiler_params=PARAMS,
    )(parts, weights)


def solution(mesh):
    in_specs = (
        P("tm", "member", "space"),
        P("member", "space"),
        P("tm", "space", None, None, None),
        P("tm", "space", None, None, None),
        P("tm", "space", "member", None, None),
        P("tm", "space", "member", None, None),
        P("tm", "space", "member", None),
    )
    out_specs = P("member", "space")
    return jax.shard_map(shards, mesh=mesh, in_specs=in_specs, out_specs=out_specs, check_vma=False)
```

```python
import math

import jax
import jax.numpy as jnp
from jax import lax
from jax.experimental import pallas as pl
from jax.experimental.pallas import tpu as pltpu
from jax.sharding import PartitionSpec as P

BLOCK = 256
LANES = 128
FIRST = {"space": 13, "member": 4, "tm": 2}
VMEM = pl.BlockSpec(memory_space=pltpu.VMEM)
HBM = pl.BlockSpec(memory_space=pltpu.HBM)
PARAMS = pltpu.CompilerParams(vmem_limit_bytes=32 * 1024 * 1024)
F32, BF16 = jnp.float32, jnp.bfloat16


def turned(rows, first):
    return jnp.concatenate([rows[first:], rows[:first]], axis=0) if first else rows


def exchange(pieces, axis):
    size = lax.axis_size(axis)
    order = [(FIRST[axis] + i) % size for i in range(size)]
    return lax.all_to_all(pieces, axis, 0, 0, tiled=True, axis_index_groups=[order])


def fetch(sems, *pairs):
    copies = [pltpu.make_async_copy(src, dst, sems.at[i]) for i, (src, dst) in enumerate(pairs)]
    for copy in copies:
        copy.start()
    return copies


def owned_kernel(innov_hbm, var_hbm, count_hbm, out_ref, innov_ref, var_ref, count_ref, sems):
    copies = fetch(sems, (count_hbm, count_ref), (var_hbm, var_ref), (innov_hbm, innov_ref))
    slots, tiles, cap = innov_ref.shape
    diag = lax.broadcasted_iota(jnp.int32, (tiles, tiles), 0) == lax.broadcasted_iota(
        jnp.int32, (tiles, tiles), 1
    )
    lane = lax.broadcasted_iota(jnp.int32, (tiles, cap), 1).astype(F32)
    copies[0].wait()
    columns = []
    for t in range(slots):
        row = count_ref[t : t + 1, :].astype(F32)
        columns.append(jnp.sum(jnp.where(diag, row, 0.0), axis=1, keepdims=True))
    copies[1].wait()
    copies[2].wait()
    rows = jnp.concatenate(
        [jnp.where(lane < columns[t], var_ref[t], 0.0) for t in range(slots)]
        + [innov_ref[t] for t in range(slots)],
        axis=1,
    )
    out_ref[...] = turned(rows, FIRST["space"])


def hot_rows(ids, count):
    iota = lax.broadcasted_iota(jnp.int32, (count, LANES), 0)
    return jnp.concatenate(
        [(iota == ids[r : r + 1]).astype(F32) for r in range(ids.shape[0])], axis=1
    )


def pick_kernel(
    scale, ens_hbm, w_hbm, fb_hbm, fo_hbm, pick_ref, hot_ref, high_ref,
    ens_ref, w_ref, fb_ref, fo_ref, low, field, split, sems,
):
    copies = fetch(sems, (fo_hbm, fo_ref), (fb_hbm, fb_ref), (w_hbm, w_ref), (ens_hbm, ens_ref))
    slots, members, cells = ens_ref.shape
    blocks = cells // BLOCK
    highs = cells // LANES
    tiles, groups, cap = fb_ref.shape[1:]
    quarters = LANES // cap
    a_rows = tiles // quarters
    copies[0].wait()
    copies[1].wait()
    for t in range(slots):
        for a in range(tiles):
            rows = pl.ds((t * a_rows + a % a_rows) * groups, groups)
            lanes = slice((a // a_rows) * cap, (a // a_rows + 1) * cap)
            offset = fo_ref[t, a]
            upper_half = offset >= LANES
            high_ref[rows, lanes] = fb_ref[t, a] + jnp.where(upper_half, blocks, 0)
            low[rows, lanes] = jnp.where(upper_half, offset - LANES, offset)
    copies[2].wait()
    copies[3].wait()
    w = w_ref[...].astype(BF16).astype(F32)
    for b in range(blocks):
        column = w[:, b : b + 1]
        for t in range(slots):
            e = ens_ref[t, :, b * BLOCK : (b + 1) * BLOCK].astype(F32)
            sums = jnp.sum(e * column, axis=0, keepdims=True)
            field[t, b : b + 1, :] = sums[:, :LANES]
            field[t, blocks + b : blocks + b + 1, :] = sums[:, LANES:]
    for t in range(slots):
        f = field[t] * scale
        upper = f.astype(BF16)
        split[t, :highs, :] = upper
        split[t, highs:, :] = (f - upper.astype(F32)).astype(BF16)

    @pl.loop(0, slots * a_rows)
    def _(step):
        base = pl.multiple_of(step * groups, groups)
        hot = hot_rows(low[pl.ds(base, groups), :], LANES).astype(BF16)
        hot_ref[step] = hot.T
        proj = jnp.dot(split[step // a_rows], hot, preferred_element_type=F32)
        own = hot_rows(high_ref[pl.ds(base, groups), :], highs)
        picked = jnp.sum(own * (proj[:highs] + proj[highs:]), axis=0, keepdims=True)
        pick_ref[pl.ds(base, groups), :] = jnp.concatenate(
            [picked[:, r * LANES : (r + 1) * LANES] for r in range(groups)], axis=0
        )


def join_kernel(pick_ref, owned_ref, out_ref):
    groups = out_ref.shape[0]
    rows = pick_ref.shape[0]
    tiles = owned_ref.shape[0]
    a_rows = (out_ref.shape[1] - rows) // 2
    quarters = tiles // a_rows
    cap = LANES // quarters
    slots = rows // (a_rows * groups)
    quarter = lax.broadcasted_iota(jnp.int32, (a_rows, LANES), 1) // cap
    sublane = lax.broadcasted_iota(jnp.int32, (groups, LANES), 0)
    own_group = sublane == lax.axis_index("member")

    owned = turned(owned_ref[...], (tiles - FIRST["space"]) % tiles)

    def aligned(source):
        total = None
        for q in range(quarters):
            part = owned[q * a_rows : (q + 1) * a_rows]
            shift = (q - source) * cap % LANES
            part = pltpu.roll(part, shift, 1) if shift else part
            total = part if total is None else jnp.where(quarter == q, part, total)
        return total

    weights = jnp.concatenate([aligned(t) for t in range(slots)], axis=0)
    for t in range(slots):
        innov = aligned(slots + t)
        for a in range(a_rows):
            at = slice((t * a_rows + a) * groups, (t * a_rows + a + 1) * groups)
            value = pick_ref[at, :] - jnp.where(own_group, innov[a : a + 1], 0.0)
            for peer in range(groups):
                out_ref[peer, at, :] = value
    for peer in range(groups):
        out_ref[peer, rows:, :] = weights


def gradient_kernel(ens_ref, got_ref, hot_ref, high_ref, out_ref):
    slots, members, cells = ens_ref.shape
    blocks = cells // BLOCK
    highs = cells // LANES
    groups = got_ref.shape[0]
    rows = high_ref.shape[0]
    a_rows = rows // (slots * groups)
    sums = [None] * blocks
    for t in range(slots):
        total = jnp.zeros((2 * highs, LANES), F32)
        for step in range(t * a_rows, (t + 1) * a_rows):
            at = slice(step * groups, (step + 1) * groups)
            value = got_ref[0, at, :]
            for peer in range(1, groups):
                value = value + got_ref[peer, at, :]
            value = value * turned(got_ref[:, rows + step, :], (groups - FIRST["member"]) % groups)
            upper = value.astype(BF16)
            lower = (value - upper.astype(F32)).astype(BF16)
            own = hot_rows(high_ref[at, :], highs).astype(BF16)
            both = jnp.concatenate(
                [
                    jnp.concatenate(
                        [
                            own[:, r * LANES : (r + 1) * LANES] * part[r : r + 1]
                            for r in range(groups)
                        ],
                        axis=1,
                    )
                    for part in (upper, lower)
                ],
                axis=0,
            )
            total += jnp.dot(both, hot_ref[step], preferred_element_type=F32)
        adjoint = (total[:highs] + total[highs:]).astype(BF16)
        adjoint = jnp.concatenate([adjoint[:blocks], adjoint[blocks:]], axis=1)
        adjoint = adjoint.astype(F32)
        for b in range(blocks):
            e = ens_ref[t, :, b * BLOCK : (b + 1) * BLOCK].astype(F32) * adjoint[b : b + 1]
            e = e[:, :LANES] + e[:, LANES:]
            sums[b] = e if t == 0 else sums[b] + e
    local = jnp.concatenate([jnp.sum(e, axis=1, keepdims=True) for e in sums], axis=1)
    height = out_ref.shape[1]
    dense = jnp.concatenate(
        [local[r : r + height] for r in range(0, members, height)], axis=1
    )
    for peer in range(out_ref.shape[0]):
        out_ref[peer] = dense


def finish_kernel(scale, got_ref, w_ref, out_ref):
    total = got_ref[0]
    for peer in range(1, got_ref.shape[0]):
        total = total + got_ref[peer]
    blocks = w_ref.shape[1]
    total = jnp.concatenate(
        [total[:, c : c + blocks] for c in range(0, LANES, blocks)], axis=0
    )
    out_ref[...] = w_ref[...] + scale * total


def cost(flops, read):
    return pl.CostEstimate(flops=flops, bytes_accessed=read, transcendentals=0)


def in_hbm(array):
    return pltpu.with_memory_space_constraint(array, pltpu.HBM)


def in_vmem(shape, dtype):
    return pltpu.VMEM(shape, dtype)


def shards(ens_pert, weights, foot_block, foot_offset, innovation, inv_var, obs_count):
    groups = lax.axis_size("member")
    windows = lax.axis_size("tm")
    slots, members, cells = ens_pert.shape
    blocks = cells // BLOCK
    highs = cells // LANES
    tiles, _, cap = foot_block.shape[2:]
    rows = slots * tiles * groups * cap // LANES
    steps = rows // groups
    scale = 1.0 / math.sqrt(members * groups - 1)
    owned = pl.pallas_call(
        owned_kernel,
        out_shape=jax.ShapeDtypeStruct((tiles, LANES), F32),
        in_specs=[HBM] * 3,
        out_specs=VMEM,
        scratch_shapes=[
            pltpu.VMEM((slots, tiles, cap), F32),
            pltpu.VMEM((slots, tiles, cap), F32),
            pltpu.VMEM((slots, tiles), jnp.int32),
            pltpu.SemaphoreType.DMA((3,)),
        ],
        compiler_params=PARAMS,
    )(
        in_hbm(innovation.reshape(slots, tiles, cap)),
        in_hbm(inv_var.reshape(slots, tiles, cap)),
        in_hbm(obs_count.reshape(slots, tiles)),
    )
    owned = exchange(owned, "space")
    picks, hot, high = pl.pallas_call(
        lambda *refs: pick_kernel(scale, *refs),
        out_shape=(
            in_vmem((rows, LANES), F32),
            in_vmem((steps, groups * LANES, LANES), BF16),
            in_vmem((rows, LANES), jnp.int32),
        ),
        in_specs=[HBM] * 4,
        out_specs=(VMEM,) * 3,
        scratch_shapes=[
            pltpu.VMEM(ens_pert.shape, BF16),
            pltpu.VMEM(weights.shape, F32),
            pltpu.VMEM((slots, tiles, groups, cap), jnp.int32),
            pltpu.VMEM((slots, tiles, groups, cap), jnp.int32),
            pltpu.VMEM((rows, LANES), jnp.int32),
            pltpu.VMEM((slots, highs, LANES), F32),
            pltpu.VMEM((slots, 2 * highs, LANES), BF16),
            pltpu.SemaphoreType.DMA((4,)),
        ],
        compiler_params=PARAMS,
        cost_estimate=cost(4 * blocks * rows * LANES * BLOCK, 4 << 20),
    )(
        in_hbm(ens_pert),
        in_hbm(weights),
        in_hbm(foot_block.reshape(slots, tiles, groups, cap)),
        in_hbm(foot_offset.reshape(slots, tiles, groups, cap)),
    )
    joined = pl.pallas_call(
        join_kernel,
        out_shape=jax.ShapeDtypeStruct((groups, rows + steps, LANES), F32),
        in_specs=[VMEM] * 2,
        out_specs=VMEM,
        compiler_params=PARAMS,
    )(picks, owned)
    got = exchange(joined, "member")
    local = pl.pallas_call(
        gradient_kernel,
        out_shape=jax.ShapeDtypeStruct((windows, members * blocks // LANES, LANES), F32),
        in_specs=[VMEM] * 4,
        out_specs=VMEM,
        compiler_params=PARAMS,
    )(ens_pert, got, hot, high)
    parts = exchange(local, "tm")
    return pl.pallas_call(
        lambda *refs: finish_kernel(scale, *refs),
        out_shape=jax.ShapeDtypeStruct(weights.shape, F32),
        in_specs=[VMEM] * 2,
        out_specs=VMEM,
        compiler_params=PARAMS,
    )(parts, weights)


def solution(mesh):
    in_specs = (
        P("tm", "member", "space"),
        P("member", "space"),
        P("tm", "space", None, None, None),
        P("tm", "space", None, None, None),
        P("tm", "space", "member", None, None),
        P("tm", "space", "member", None, None),
        P("tm", "space", "member", None),
    )
    out_specs = P("member", "space")
    return jax.shard_map(shards, mesh=mesh, in_specs=in_specs, out_specs=out_specs, check_vma=False)
```

```python
import math

import jax
import jax.numpy as jnp
from jax import lax
from jax.experimental import pallas as pl
from jax.experimental.pallas import tpu as pltpu
from jax.sharding import PartitionSpec as P

BLOCK = 256
LANES = 128
FIRST = {"space": 11, "member": 5, "tm": 2}
VMEM = pl.BlockSpec(memory_space=pltpu.VMEM)
HBM = pl.BlockSpec(memory_space=pltpu.HBM)
PARAMS = pltpu.CompilerParams(vmem_limit_bytes=32 * 1024 * 1024)
F32, BF16 = jnp.float32, jnp.bfloat16


def turned(rows, first):
    return jnp.concatenate([rows[first:], rows[:first]], axis=0) if first else rows


def exchange(pieces, axis):
    size = lax.axis_size(axis)
    order = [(FIRST[axis] + i) % size for i in range(size)]
    return lax.all_to_all(pieces, axis, 0, 0, tiled=True, axis_index_groups=[order])


def fetch(sems, *pairs):
    copies = [pltpu.make_async_copy(src, dst, sems.at[i]) for i, (src, dst) in enumerate(pairs)]
    for copy in copies:
        copy.start()
    return copies


def owned_kernel(
    innov_hbm, var_hbm, count_hbm, fb_hbm, fo_hbm, w_hbm, ens_hbm,
    out_hbm, fb_ref, fo_ref, w_ref, ens_ref, innov_ref, var_ref, count_ref, out_ref, sems,
):
    copies = fetch(
        sems,
        (count_hbm, count_ref),
        (var_hbm, var_ref),
        (innov_hbm, innov_ref),
        (fo_hbm, fo_ref),
        (fb_hbm, fb_ref),
        (w_hbm, w_ref),
        (ens_hbm, ens_ref),
    )
    slots, tiles, cap = innov_ref.shape
    diag = lax.broadcasted_iota(jnp.int32, (tiles, tiles), 0) == lax.broadcasted_iota(
        jnp.int32, (tiles, tiles), 1
    )
    lane = lax.broadcasted_iota(jnp.int32, (tiles, cap), 1).astype(F32)
    copies[0].wait()
    columns = []
    for t in range(slots):
        row = count_ref[t : t + 1, :].astype(F32)
        columns.append(jnp.sum(jnp.where(diag, row, 0.0), axis=1, keepdims=True))
    copies[1].wait()
    copies[2].wait()
    rows = jnp.concatenate(
        [jnp.where(lane < columns[t], var_ref[t], 0.0) for t in range(slots)]
        + [innov_ref[t] for t in range(slots)],
        axis=1,
    )
    out_ref[...] = turned(rows, FIRST["space"])
    write = pltpu.make_async_copy(out_ref, out_hbm, sems.at[len(copies)])
    write.start()
    for copy in copies[3:]:
        copy.wait()
    write.wait()


def hot_rows(ids, count):
    iota = lax.broadcasted_iota(jnp.int32, (count, LANES), 0)
    return jnp.concatenate(
        [(iota == ids[r : r + 1]).astype(F32) for r in range(ids.shape[0])], axis=1
    )


def pick_kernel(
    scale, ens_ref, w_ref, fb_ref, fo_ref, pick_ref, hot_ref, high_ref, low, field, split
):
    slots, members, cells = ens_ref.shape
    blocks = cells // BLOCK
    highs = cells // LANES
    tiles, groups, cap = fb_ref.shape[1:]
    quarters = LANES // cap
    a_rows = tiles // quarters
    for t in range(slots):
        for a in range(tiles):
            rows = pl.ds((t * a_rows + a % a_rows) * groups, groups)
            lanes = slice((a // a_rows) * cap, (a // a_rows + 1) * cap)
            offset = fo_ref[t, a]
            upper_half = offset >= LANES
            high_ref[rows, lanes] = fb_ref[t, a] + jnp.where(upper_half, blocks, 0)
            low[rows, lanes] = jnp.where(upper_half, offset - LANES, offset)
    w = w_ref[...].astype(BF16).astype(F32)
    for b in range(blocks):
        column = w[:, b : b + 1]
        for t in range(slots):
            e = ens_ref[t, :, b * BLOCK : (b + 1) * BLOCK].astype(F32)
            sums = jnp.sum(e * column, axis=0, keepdims=True)
            field[t, b : b + 1, :] = sums[:, :LANES]
            field[t, blocks + b : blocks + b + 1, :] = sums[:, LANES:]
    for t in range(slots):
        f = field[t] * scale
        upper = f.astype(BF16)
        split[t, :highs, :] = upper
        split[t, highs:, :] = (f - upper.astype(F32)).astype(BF16)

    @pl.loop(0, slots * a_rows)
    def _(step):
        base = pl.multiple_of(step * groups, groups)
        hot = hot_rows(low[pl.ds(base, groups), :], LANES).astype(BF16)
        hot_ref[step] = hot.T
        proj = jnp.dot(split[step // a_rows], hot, preferred_element_type=F32)
        own = hot_rows(high_ref[pl.ds(base, groups), :], highs)
        picked = jnp.sum(own * (proj[:highs] + proj[highs:]), axis=0, keepdims=True)
        pick_ref[pl.ds(base, groups), :] = jnp.concatenate(
            [picked[:, r * LANES : (r + 1) * LANES] for r in range(groups)], axis=0
        )


def join_kernel(pick_ref, owned_ref, out_ref):
    groups = out_ref.shape[0]
    rows = pick_ref.shape[0]
    tiles = owned_ref.shape[0]
    a_rows = (out_ref.shape[1] - rows) // 2
    quarters = tiles // a_rows
    cap = LANES // quarters
    slots = rows // (a_rows * groups)
    quarter = lax.broadcasted_iota(jnp.int32, (a_rows, LANES), 1) // cap
    sublane = lax.broadcasted_iota(jnp.int32, (groups, LANES), 0)
    own_group = sublane == lax.axis_index("member")

    owned = turned(owned_ref[...], (tiles - FIRST["space"]) % tiles)

    def aligned(source):
        total = None
        for q in range(quarters):
            part = owned[q * a_rows : (q + 1) * a_rows]
            shift = (q - source) * cap % LANES
            part = pltpu.roll(part, shift, 1) if shift else part
            total = part if total is None else jnp.where(quarter == q, part, total)
        return total

    weights = jnp.concatenate([aligned(t) for t in range(slots)], axis=0)
    for t in range(slots):
        innov = aligned(slots + t)
        for a in range(a_rows):
            at = slice((t * a_rows + a) * groups, (t * a_rows + a + 1) * groups)
            value = pick_ref[at, :] - jnp.where(own_group, innov[a : a + 1], 0.0)
            for peer in range(groups):
                out_ref[peer, at, :] = value
    for peer in range(groups):
        out_ref[peer, rows:, :] = weights


def gradient_kernel(ens_ref, got_ref, hot_ref, high_ref, out_ref):
    slots, members, cells = ens_ref.shape
    blocks = cells // BLOCK
    highs = cells // LANES
    groups = got_ref.shape[0]
    rows = high_ref.shape[0]
    a_rows = rows // (slots * groups)
    sums = [None] * blocks
    for t in range(slots):
        total = jnp.zeros((2 * highs, LANES), F32)
        for step in range(t * a_rows, (t + 1) * a_rows):
            at = slice(step * groups, (step + 1) * groups)
            value = got_ref[0, at, :]
            for peer in range(1, groups):
                value = value + got_ref[peer, at, :]
            value = value * turned(got_ref[:, rows + step, :], (groups - FIRST["member"]) % groups)
            upper = value.astype(BF16)
            lower = (value - upper.astype(F32)).astype(BF16)
            own = hot_rows(high_ref[at, :], highs).astype(BF16)
            both = jnp.concatenate(
                [
                    jnp.concatenate(
                        [
                            own[:, r * LANES : (r + 1) * LANES] * part[r : r + 1]
                            for r in range(groups)
                        ],
                        axis=1,
                    )
                    for part in (upper, lower)
                ],
                axis=0,
            )
            total += jnp.dot(both, hot_ref[step], preferred_element_type=F32)
        adjoint = (total[:highs] + total[highs:]).astype(BF16)
        adjoint = jnp.concatenate([adjoint[:blocks], adjoint[blocks:]], axis=1)
        adjoint = adjoint.astype(F32)
        for b in range(blocks):
            e = ens_ref[t, :, b * BLOCK : (b + 1) * BLOCK].astype(F32) * adjoint[b : b + 1]
            e = e[:, :LANES] + e[:, LANES:]
            sums[b] = e if t == 0 else sums[b] + e
    local = jnp.concatenate([jnp.sum(e, axis=1, keepdims=True) for e in sums], axis=1)
    height = out_ref.shape[1]
    dense = jnp.concatenate(
        [local[r : r + height] for r in range(0, members, height)], axis=1
    )
    for peer in range(out_ref.shape[0]):
        out_ref[peer] = dense


def finish_kernel(scale, got_ref, w_ref, out_ref):
    total = got_ref[0]
    for peer in range(1, got_ref.shape[0]):
        total = total + got_ref[peer]
    blocks = w_ref.shape[1]
    total = jnp.concatenate(
        [total[:, c : c + blocks] for c in range(0, LANES, blocks)], axis=0
    )
    out_ref[...] = w_ref[...] + scale * total


def cost(flops, read):
    return pl.CostEstimate(flops=flops, bytes_accessed=read, transcendentals=0)


def in_hbm(array):
    return pltpu.with_memory_space_constraint(array, pltpu.HBM)


def in_vmem(shape, dtype):
    return pltpu.VMEM(shape, dtype)


def shards(ens_pert, weights, foot_block, foot_offset, innovation, inv_var, obs_count):
    groups = lax.axis_size("member")
    windows = lax.axis_size("tm")
    slots, members, cells = ens_pert.shape
    blocks = cells // BLOCK
    highs = cells // LANES
    tiles, _, cap = foot_block.shape[2:]
    rows = slots * tiles * groups * cap // LANES
    steps = rows // groups
    scale = 1.0 / math.sqrt(members * groups - 1)
    owned, fb, fo, w, ens = pl.pallas_call(
        owned_kernel,
        out_shape=(
            jax.ShapeDtypeStruct((tiles, LANES), F32),
            in_vmem((slots, tiles, groups, cap), jnp.int32),
            in_vmem((slots, tiles, groups, cap), jnp.int32),
            in_vmem(weights.shape, F32),
            in_vmem(ens_pert.shape, BF16),
        ),
        in_specs=[HBM] * 7,
        out_specs=(HBM,) + (VMEM,) * 4,
        scratch_shapes=[
            pltpu.VMEM((slots, tiles, cap), F32),
            pltpu.VMEM((slots, tiles, cap), F32),
            pltpu.VMEM((slots, tiles), jnp.int32),
            pltpu.VMEM((tiles, LANES), F32),
            pltpu.SemaphoreType.DMA((8,)),
        ],
        compiler_params=PARAMS,
    )(
        in_hbm(innovation.reshape(slots, tiles, cap)),
        in_hbm(inv_var.reshape(slots, tiles, cap)),
        in_hbm(obs_count.reshape(slots, tiles)),
        in_hbm(foot_block.reshape(slots, tiles, groups, cap)),
        in_hbm(foot_offset.reshape(slots, tiles, groups, cap)),
        in_hbm(weights),
        in_hbm(ens_pert),
    )
    owned = exchange(owned, "space")
    picks, hot, high = pl.pallas_call(
        lambda *refs: pick_kernel(scale, *refs),
        out_shape=(
            in_vmem((rows, LANES), F32),
            in_vmem((steps, groups * LANES, LANES), BF16),
            in_vmem((rows, LANES), jnp.int32),
        ),
        in_specs=[VMEM] * 4,
        out_specs=(VMEM,) * 3,
        scratch_shapes=[
            pltpu.VMEM((rows, LANES), jnp.int32),
            pltpu.VMEM((slots, highs, LANES), F32),
            pltpu.VMEM((slots, 2 * highs, LANES), BF16),
        ],
        compiler_params=PARAMS,
        cost_estimate=cost(4 * blocks * rows * LANES * BLOCK, 4 << 20),
    )(ens, w, fb, fo)
    joined = pl.pallas_call(
        join_kernel,
        out_shape=jax.ShapeDtypeStruct((groups, rows + steps, LANES), F32),
        in_specs=[VMEM] * 2,
        out_specs=VMEM,
        compiler_params=PARAMS,
    )(picks, owned)
    got = exchange(joined, "member")
    local = pl.pallas_call(
        gradient_kernel,
        out_shape=jax.ShapeDtypeStruct((windows, members * blocks // LANES, LANES), F32),
        in_specs=[VMEM] * 4,
        out_specs=VMEM,
        compiler_params=PARAMS,
    )(ens, got, hot, high)
    parts = exchange(local, "tm")
    return pl.pallas_call(
        lambda *refs: finish_kernel(scale, *refs),
        out_shape=jax.ShapeDtypeStruct(weights.shape, F32),
        in_specs=[VMEM] * 2,
        out_specs=VMEM,
        compiler_params=PARAMS,
    )(parts, w)


def solution(mesh):
    in_specs = (
        P("tm", "member", "space"),
        P("member", "space"),
        P("tm", "space", None, None, None),
        P("tm", "space", None, None, None),
        P("tm", "space", "member", None, None),
        P("tm", "space", "member", None, None),
        P("tm", "space", "member", None),
    )
    out_specs = P("member", "space")
    return jax.shard_map(shards, mesh=mesh, in_specs=in_specs, out_specs=out_specs, check_vma=False)
```

```python
import math

import jax
import jax.numpy as jnp
from jax import lax
from jax.experimental import pallas as pl
from jax.experimental.pallas import tpu as pltpu
from jax.sharding import PartitionSpec as P

BLOCK = 256
LANES = 128
FIRST = {"space": 11, "member": 5, "tm": 2}
VMEM = pl.BlockSpec(memory_space=pltpu.VMEM)
HBM = pl.BlockSpec(memory_space=pltpu.HBM)
PARAMS = pltpu.CompilerParams(vmem_limit_bytes=32 * 1024 * 1024)
F32, BF16 = jnp.float32, jnp.bfloat16


def turned(rows, first):
    return jnp.concatenate([rows[first:], rows[:first]], axis=0) if first else rows


def exchange(pieces, axis):
    size = lax.axis_size(axis)
    order = [(FIRST[axis] + i) % size for i in range(size)]
    return lax.all_to_all(pieces, axis, 0, 0, tiled=True, axis_index_groups=[order])


def fetch(sems, *pairs):
    copies = [pltpu.make_async_copy(src, dst, sems.at[i]) for i, (src, dst) in enumerate(pairs)]
    for copy in copies:
        copy.start()
    return copies


def owned_kernel(
    innov_hbm, var_hbm, count_hbm, fb_hbm, fo_hbm, w_hbm, ens_hbm,
    out_hbm, fb_ref, fo_ref, w_ref, ens_ref, innov_ref, var_ref, count_ref, out_ref, sems,
):
    copies = fetch(sems, (count_hbm, count_ref), (var_hbm, var_ref), (innov_hbm, innov_ref))
    slots, tiles, cap = innov_ref.shape
    diag = lax.broadcasted_iota(jnp.int32, (tiles, tiles), 0) == lax.broadcasted_iota(
        jnp.int32, (tiles, tiles), 1
    )
    lane = lax.broadcasted_iota(jnp.int32, (tiles, cap), 1).astype(F32)
    copies[0].wait()
    columns = []
    for t in range(slots):
        row = count_ref[t : t + 1, :].astype(F32)
        columns.append(jnp.sum(jnp.where(diag, row, 0.0), axis=1, keepdims=True))
    copies[1].wait()
    copies[2].wait()
    first = FIRST["space"]
    for t in range(slots):
        held = jnp.where(lane < columns[t], var_ref[t], 0.0)
        out_ref[:, t * cap : (t + 1) * cap] = turned(held, first)
        given = turned(innov_ref[t], first)
        out_ref[:, (slots + t) * cap : (slots + t + 1) * cap] = given
    write = pltpu.make_async_copy(out_ref, out_hbm, sems.at[7])
    write.start()
    pairs = ((fo_hbm, fo_ref), (fb_hbm, fb_ref), (w_hbm, w_ref), (ens_hbm, ens_ref))
    rest = [pltpu.make_async_copy(src, dst, sems.at[3 + i]) for i, (src, dst) in enumerate(pairs)]
    for copy in rest:
        copy.start()
    for copy in rest:
        copy.wait()
    write.wait()


def hot_rows(ids, count):
    iota = lax.broadcasted_iota(jnp.int32, (count, LANES), 0)
    return jnp.concatenate(
        [(iota == ids[r : r + 1]).astype(F32) for r in range(ids.shape[0])], axis=1
    )


def pick_kernel(
    scale, ens_ref, w_ref, fb_ref, fo_ref, pick_ref, hot_ref, high_ref, low, field, split
):
    slots, members, cells = ens_ref.shape
    blocks = cells // BLOCK
    highs = cells // LANES
    tiles, groups, cap = fb_ref.shape[1:]
    quarters = LANES // cap
    a_rows = tiles // quarters
    for t in range(slots):
        for a in range(tiles):
            rows = pl.ds((t * a_rows + a % a_rows) * groups, groups)
            lanes = slice((a // a_rows) * cap, (a // a_rows + 1) * cap)
            offset = fo_ref[t, a]
            upper_half = offset >= LANES
            high_ref[rows, lanes] = fb_ref[t, a] + jnp.where(upper_half, blocks, 0)
            low[rows, lanes] = jnp.where(upper_half, offset - LANES, offset)
    w = w_ref[...].astype(BF16).astype(F32)
    for b in range(blocks):
        column = w[:, b : b + 1]
        for t in range(slots):
            e = ens_ref[t, :, b * BLOCK : (b + 1) * BLOCK].astype(F32)
            sums = jnp.sum(e * column, axis=0, keepdims=True)
            field[t, b : b + 1, :] = sums[:, :LANES]
            field[t, blocks + b : blocks + b + 1, :] = sums[:, LANES:]
    for t in range(slots):
        f = field[t] * scale
        upper = f.astype(BF16)
        split[t, :highs, :] = upper
        split[t, highs:, :] = (f - upper.astype(F32)).astype(BF16)

    @pl.loop(0, slots * a_rows)
    def _(step):
        base = pl.multiple_of(step * groups, groups)
        hot = hot_rows(low[pl.ds(base, groups), :], LANES).astype(BF16)
        hot_ref[step] = hot.T
        proj = jnp.dot(split[step // a_rows], hot, preferred_element_type=F32)
        own = hot_rows(high_ref[pl.ds(base, groups), :], highs)
        picked = jnp.sum(own * (proj[:highs] + proj[highs:]), axis=0, keepdims=True)
        pick_ref[pl.ds(base, groups), :] = jnp.concatenate(
            [picked[:, r * LANES : (r + 1) * LANES] for r in range(groups)], axis=0
        )


def join_kernel(pick_ref, owned_ref, out_ref):
    groups = out_ref.shape[0]
    rows = pick_ref.shape[0]
    tiles = owned_ref.shape[0]
    a_rows = (out_ref.shape[1] - rows) // 2
    quarters = tiles // a_rows
    cap = LANES // quarters
    slots = rows // (a_rows * groups)
    quarter = lax.broadcasted_iota(jnp.int32, (a_rows, LANES), 1) // cap
    sublane = lax.broadcasted_iota(jnp.int32, (groups, LANES), 0)
    own_group = sublane == lax.axis_index("member")

    owned = turned(owned_ref[...], (tiles - FIRST["space"]) % tiles)

    def aligned(source):
        total = None
        for q in range(quarters):
            part = owned[q * a_rows : (q + 1) * a_rows]
            shift = (q - source) * cap % LANES
            part = pltpu.roll(part, shift, 1) if shift else part
            total = part if total is None else jnp.where(quarter == q, part, total)
        return total

    weights = jnp.concatenate([aligned(t) for t in range(slots)], axis=0)
    for t in range(slots):
        innov = aligned(slots + t)
        for a in range(a_rows):
            at = slice((t * a_rows + a) * groups, (t * a_rows + a + 1) * groups)
            value = pick_ref[at, :] - jnp.where(own_group, innov[a : a + 1], 0.0)
            for peer in range(groups):
                out_ref[peer, at, :] = value
    for peer in range(groups):
        out_ref[peer, rows:, :] = weights


def gradient_kernel(ens_ref, got_ref, hot_ref, high_ref, out_ref):
    slots, members, cells = ens_ref.shape
    blocks = cells // BLOCK
    highs = cells // LANES
    groups = got_ref.shape[0]
    rows = high_ref.shape[0]
    a_rows = rows // (slots * groups)
    sums = [None] * blocks
    for t in range(slots):
        total = jnp.zeros((2 * highs, LANES), F32)
        for step in range(t * a_rows, (t + 1) * a_rows):
            at = slice(step * groups, (step + 1) * groups)
            value = got_ref[0, at, :]
            for peer in range(1, groups):
                value = value + got_ref[peer, at, :]
            value = value * turned(got_ref[:, rows + step, :], (groups - FIRST["member"]) % groups)
            upper = value.astype(BF16)
            lower = (value - upper.astype(F32)).astype(BF16)
            own = hot_rows(high_ref[at, :], highs).astype(BF16)
            both = jnp.concatenate(
                [
                    jnp.concatenate(
                        [
                            own[:, r * LANES : (r + 1) * LANES] * part[r : r + 1]
                            for r in range(groups)
                        ],
                        axis=1,
                    )
                    for part in (upper, lower)
                ],
                axis=0,
            )
            total += jnp.dot(both, hot_ref[step], preferred_element_type=F32)
        adjoint = (total[:highs] + total[highs:]).astype(BF16)
        adjoint = jnp.concatenate([adjoint[:blocks], adjoint[blocks:]], axis=1)
        adjoint = adjoint.astype(F32)
        for b in range(blocks):
            e = ens_ref[t, :, b * BLOCK : (b + 1) * BLOCK].astype(F32) * adjoint[b : b + 1]
            e = e[:, :LANES] + e[:, LANES:]
            sums[b] = e if t == 0 else sums[b] + e
    local = jnp.concatenate([jnp.sum(e, axis=1, keepdims=True) for e in sums], axis=1)
    height = out_ref.shape[1]
    dense = jnp.concatenate(
        [local[r : r + height] for r in range(0, members, height)], axis=1
    )
    for peer in range(out_ref.shape[0]):
        out_ref[peer] = dense


def finish_kernel(scale, got_ref, w_ref, out_ref):
    total = got_ref[0]
    for peer in range(1, got_ref.shape[0]):
        total = total + got_ref[peer]
    blocks = w_ref.shape[1]
    total = jnp.concatenate(
        [total[:, c : c + blocks] for c in range(0, LANES, blocks)], axis=0
    )
    out_ref[...] = w_ref[...] + scale * total


def cost(flops, read):
    return pl.CostEstimate(flops=flops, bytes_accessed=read, transcendentals=0)


def in_hbm(array):
    return pltpu.with_memory_space_constraint(array, pltpu.HBM)


def in_vmem(shape, dtype):
    return pltpu.VMEM(shape, dtype)


def shards(ens_pert, weights, foot_block, foot_offset, innovation, inv_var, obs_count):
    groups = lax.axis_size("member")
    windows = lax.axis_size("tm")
    slots, members, cells = ens_pert.shape
    blocks = cells // BLOCK
    highs = cells // LANES
    tiles, _, cap = foot_block.shape[2:]
    rows = slots * tiles * groups * cap // LANES
    steps = rows // groups
    scale = 1.0 / math.sqrt(members * groups - 1)
    owned, fb, fo, w, ens = pl.pallas_call(
        owned_kernel,
        out_shape=(
            jax.ShapeDtypeStruct((tiles, LANES), F32),
            in_vmem((slots, tiles, groups, cap), jnp.int32),
            in_vmem((slots, tiles, groups, cap), jnp.int32),
            in_vmem(weights.shape, F32),
            in_vmem(ens_pert.shape, BF16),
        ),
        in_specs=[HBM] * 7,
        out_specs=(HBM,) + (VMEM,) * 4,
        scratch_shapes=[
            pltpu.VMEM((slots, tiles, cap), F32),
            pltpu.VMEM((slots, tiles, cap), F32),
            pltpu.VMEM((slots, tiles), jnp.int32),
            pltpu.VMEM((tiles, LANES), F32),
            pltpu.SemaphoreType.DMA((8,)),
        ],
        compiler_params=PARAMS,
    )(
        in_hbm(innovation.reshape(slots, tiles, cap)),
        in_hbm(inv_var.reshape(slots, tiles, cap)),
        in_hbm(obs_count.reshape(slots, tiles)),
        in_hbm(foot_block.reshape(slots, tiles, groups, cap)),
        in_hbm(foot_offset.reshape(slots, tiles, groups, cap)),
        in_hbm(weights),
        in_hbm(ens_pert),
    )
    owned = exchange(owned, "space")
    picks, hot, high = pl.pallas_call(
        lambda *refs: pick_kernel(scale, *refs),
        out_shape=(
            in_vmem((rows, LANES), F32),
            in_vmem((steps, groups * LANES, LANES), BF16),
            in_vmem((rows, LANES), jnp.int32),
        ),
        in_specs=[VMEM] * 4,
        out_specs=(VMEM,) * 3,
        scratch_shapes=[
            pltpu.VMEM((rows, LANES), jnp.int32),
            pltpu.VMEM((slots, highs, LANES), F32),
            pltpu.VMEM((slots, 2 * highs, LANES), BF16),
        ],
        compiler_params=PARAMS,
        cost_estimate=cost(4 * blocks * rows * LANES * BLOCK, 4 << 20),
    )(ens, w, fb, fo)
    joined = pl.pallas_call(
        join_kernel,
        out_shape=jax.ShapeDtypeStruct((groups, rows + steps, LANES), F32),
        in_specs=[VMEM] * 2,
        out_specs=VMEM,
        compiler_params=PARAMS,
    )(picks, owned)
    got = exchange(joined, "member")
    local = pl.pallas_call(
        gradient_kernel,
        out_shape=jax.ShapeDtypeStruct((windows, members * blocks // LANES, LANES), F32),
        in_specs=[VMEM] * 4,
        out_specs=VMEM,
        compiler_params=PARAMS,
    )(ens, got, hot, high)
    parts = exchange(local, "tm")
    return pl.pallas_call(
        lambda *refs: finish_kernel(scale, *refs),
        out_shape=jax.ShapeDtypeStruct(weights.shape, F32),
        in_specs=[VMEM] * 2,
        out_specs=VMEM,
        compiler_params=PARAMS,
    )(parts, w)


def solution(mesh):
    in_specs = (
        P("tm", "member", "space"),
        P("member", "space"),
        P("tm", "space", None, None, None),
        P("tm", "space", None, None, None),
        P("tm", "space", "member", None, None),
        P("tm", "space", "member", None, None),
        P("tm", "space", "member", None),
    )
    out_specs = P("member", "space")
    return jax.shard_map(shards, mesh=mesh, in_specs=in_specs, out_specs=out_specs, check_vma=False)
```

```python
import math

import jax
import jax.numpy as jnp
from jax import lax
from jax.experimental import pallas as pl
from jax.experimental.pallas import tpu as pltpu
from jax.sharding import PartitionSpec as P

BLOCK = 256
LANES = 128
FIRST = {"space": 11, "member": 5, "tm": 2}
VMEM = pl.BlockSpec(memory_space=pltpu.VMEM)
HBM = pl.BlockSpec(memory_space=pltpu.HBM)
PARAMS = pltpu.CompilerParams(vmem_limit_bytes=32 * 1024 * 1024)
F32, BF16 = jnp.float32, jnp.bfloat16


def turned(rows, first):
    return jnp.concatenate([rows[first:], rows[:first]], axis=0) if first else rows


def exchange(pieces, axis):
    size = lax.axis_size(axis)
    order = [(FIRST[axis] + i) % size for i in range(size)]
    return lax.all_to_all(pieces, axis, 0, 0, tiled=True, axis_index_groups=[order])


def fetch(sems, *pairs):
    copies = [pltpu.make_async_copy(src, dst, sems.at[i]) for i, (src, dst) in enumerate(pairs)]
    for copy in copies:
        copy.start()
    return copies


def owned_kernel(
    innov_hbm, var_hbm, count_hbm, fb_hbm, fo_hbm, w_hbm, ens_hbm,
    out_hbm, fb_ref, fo_ref, w_ref, ens_ref, innov_ref, var_ref, count_ref, out_ref, sems,
):
    copies = fetch(
        sems,
        (count_hbm, count_ref),
        (var_hbm, var_ref),
        (innov_hbm, innov_ref),
        (fo_hbm, fo_ref),
        (fb_hbm, fb_ref),
        (w_hbm, w_ref),
        (ens_hbm, ens_ref),
    )
    slots, tiles, cap = innov_ref.shape
    diag = lax.broadcasted_iota(jnp.int32, (tiles, tiles), 0) == lax.broadcasted_iota(
        jnp.int32, (tiles, tiles), 1
    )
    lane = lax.broadcasted_iota(jnp.int32, (tiles, cap), 1).astype(F32)
    copies[0].wait()
    columns = []
    for t in range(slots):
        row = count_ref[t : t + 1, :].astype(F32)
        columns.append(jnp.sum(jnp.where(diag, row, 0.0), axis=1, keepdims=True))
    copies[1].wait()
    copies[2].wait()
    first = FIRST["space"]
    for t in range(slots):
        held = jnp.where(lane < columns[t], var_ref[t], 0.0)
        out_ref[:, t * cap : (t + 1) * cap] = turned(held, first)
        given = turned(innov_ref[t], first)
        out_ref[:, (slots + t) * cap : (slots + t + 1) * cap] = given
    write = pltpu.make_async_copy(out_ref, out_hbm, sems.at[len(copies)])
    write.start()
    for copy in copies[3:]:
        copy.wait()
    write.wait()


def hot_rows(ids, count):
    iota = lax.broadcasted_iota(jnp.int32, (count, LANES), 0)
    return jnp.concatenate(
        [(iota == ids[r : r + 1]).astype(F32) for r in range(ids.shape[0])], axis=1
    )


def pick_kernel(
    scale, ens_ref, w_ref, fb_ref, fo_ref, pick_ref, hot_ref, high_ref, low, field, split
):
    slots, members, cells = ens_ref.shape
    blocks = cells // BLOCK
    highs = cells // LANES
    tiles, groups, cap = fb_ref.shape[1:]
    quarters = LANES // cap
    a_rows = tiles // quarters
    for t in range(slots):
        for a in range(tiles):
            rows = pl.ds((t * a_rows + a % a_rows) * groups, groups)
            lanes = slice((a // a_rows) * cap, (a // a_rows + 1) * cap)
            offset = fo_ref[t, a]
            upper_half = offset >= LANES
            high_ref[rows, lanes] = fb_ref[t, a] + jnp.where(upper_half, blocks, 0)
            low[rows, lanes] = jnp.where(upper_half, offset - LANES, offset)
    w = w_ref[...].astype(BF16).astype(F32)
    for b in range(blocks):
        column = w[:, b : b + 1]
        for t in range(slots):
            e = ens_ref[t, :, b * BLOCK : (b + 1) * BLOCK].astype(F32)
            sums = jnp.sum(e * column, axis=0, keepdims=True)
            field[t, b : b + 1, :] = sums[:, :LANES]
            field[t, blocks + b : blocks + b + 1, :] = sums[:, LANES:]
    for t in range(slots):
        f = field[t] * scale
        upper = f.astype(BF16)
        split[t, :highs, :] = upper
        split[t, highs:, :] = (f - upper.astype(F32)).astype(BF16)

    @pl.loop(0, slots * a_rows)
    def _(step):
        base = pl.multiple_of(step * groups, groups)
        hot = hot_rows(low[pl.ds(base, groups), :], LANES).astype(BF16)
        hot_ref[step] = hot.T
        proj = jnp.dot(split[step // a_rows], hot, preferred_element_type=F32)
        own = hot_rows(high_ref[pl.ds(base, groups), :], highs)
        picked = jnp.sum(own * (proj[:highs] + proj[highs:]), axis=0, keepdims=True)
        pick_ref[pl.ds(base, groups), :] = jnp.concatenate(
            [picked[:, r * LANES : (r + 1) * LANES] for r in range(groups)], axis=0
        )


def join_kernel(pick_ref, owned_ref, out_ref):
    groups = out_ref.shape[0]
    rows = pick_ref.shape[0]
    tiles = owned_ref.shape[0]
    a_rows = (out_ref.shape[1] - rows) // 2
    quarters = tiles // a_rows
    cap = LANES // quarters
    slots = rows // (a_rows * groups)
    quarter = lax.broadcasted_iota(jnp.int32, (a_rows, LANES), 1) // cap
    sublane = lax.broadcasted_iota(jnp.int32, (groups, LANES), 0)
    own_group = sublane == lax.axis_index("member")

    owned = turned(owned_ref[...], (tiles - FIRST["space"]) % tiles)

    def aligned(source):
        total = None
        for q in range(quarters):
            part = owned[q * a_rows : (q + 1) * a_rows]
            shift = (q - source) * cap % LANES
            part = pltpu.roll(part, shift, 1) if shift else part
            total = part if total is None else jnp.where(quarter == q, part, total)
        return total

    weights = jnp.concatenate([aligned(t) for t in range(slots)], axis=0)
    for t in range(slots):
        innov = aligned(slots + t)
        for a in range(a_rows):
            at = slice((t * a_rows + a) * groups, (t * a_rows + a + 1) * groups)
            value = pick_ref[at, :] - jnp.where(own_group, innov[a : a + 1], 0.0)
            for peer in range(groups):
                out_ref[peer, at, :] = value
    for peer in range(groups):
        out_ref[peer, rows:, :] = weights


def gradient_kernel(ens_ref, got_ref, hot_ref, high_ref, out_ref):
    slots, members, cells = ens_ref.shape
    blocks = cells // BLOCK
    highs = cells // LANES
    groups = got_ref.shape[0]
    rows = high_ref.shape[0]
    a_rows = rows // (slots * groups)
    sums = [None] * blocks
    for t in range(slots):
        total = jnp.zeros((2 * highs, LANES), F32)
        for step in range(t * a_rows, (t + 1) * a_rows):
            at = slice(step * groups, (step + 1) * groups)
            value = got_ref[0, at, :]
            for peer in range(1, groups):
                value = value + got_ref[peer, at, :]
            value = value * turned(got_ref[:, rows + step, :], (groups - FIRST["member"]) % groups)
            upper = value.astype(BF16)
            lower = (value - upper.astype(F32)).astype(BF16)
            own = hot_rows(high_ref[at, :], highs).astype(BF16)
            both = jnp.concatenate(
                [
                    jnp.concatenate(
                        [
                            own[:, r * LANES : (r + 1) * LANES] * part[r : r + 1]
                            for r in range(groups)
                        ],
                        axis=1,
                    )
                    for part in (upper, lower)
                ],
                axis=0,
            )
            total += jnp.dot(both, hot_ref[step], preferred_element_type=F32)
        adjoint = (total[:highs] + total[highs:]).astype(BF16)
        adjoint = jnp.concatenate([adjoint[:blocks], adjoint[blocks:]], axis=1)
        adjoint = adjoint.astype(F32)
        for b in range(blocks):
            e = ens_ref[t, :, b * BLOCK : (b + 1) * BLOCK].astype(F32) * adjoint[b : b + 1]
            e = e[:, :LANES] + e[:, LANES:]
            sums[b] = e if t == 0 else sums[b] + e
    local = jnp.concatenate([jnp.sum(e, axis=1, keepdims=True) for e in sums], axis=1)
    height = out_ref.shape[1]
    dense = jnp.concatenate(
        [local[r : r + height] for r in range(0, members, height)], axis=1
    )
    for peer in range(out_ref.shape[0]):
        out_ref[peer] = dense


def finish_kernel(scale, got_ref, w_ref, out_ref):
    total = got_ref[0]
    for peer in range(1, got_ref.shape[0]):
        total = total + got_ref[peer]
    blocks = w_ref.shape[1]
    total = jnp.concatenate(
        [total[:, c : c + blocks] for c in range(0, LANES, blocks)], axis=0
    )
    out_ref[...] = w_ref[...] + scale * total


def cost(flops, read):
    return pl.CostEstimate(flops=flops, bytes_accessed=read, transcendentals=0)


def in_hbm(array):
    return pltpu.with_memory_space_constraint(array, pltpu.HBM)


def in_vmem(shape, dtype):
    return pltpu.VMEM(shape, dtype)


def shards(ens_pert, weights, foot_block, foot_offset, innovation, inv_var, obs_count):
    groups = lax.axis_size("member")
    windows = lax.axis_size("tm")
    slots, members, cells = ens_pert.shape
    blocks = cells // BLOCK
    highs = cells // LANES
    tiles, _, cap = foot_block.shape[2:]
    rows = slots * tiles * groups * cap // LANES
    steps = rows // groups
    scale = 1.0 / math.sqrt(members * groups - 1)
    owned, fb, fo, w, ens = pl.pallas_call(
        owned_kernel,
        out_shape=(
            jax.ShapeDtypeStruct((tiles, LANES), F32),
            in_vmem((slots, tiles, groups, cap), jnp.int32),
            in_vmem((slots, tiles, groups, cap), jnp.int32),
            in_vmem(weights.shape, F32),
            in_vmem(ens_pert.shape, BF16),
        ),
        in_specs=[HBM] * 7,
        out_specs=(HBM,) + (VMEM,) * 4,
        scratch_shapes=[
            pltpu.VMEM((slots, tiles, cap), F32),
            pltpu.VMEM((slots, tiles, cap), F32),
            pltpu.VMEM((slots, tiles), jnp.int32),
            pltpu.VMEM((tiles, LANES), F32),
            pltpu.SemaphoreType.DMA((8,)),
        ],
        compiler_params=PARAMS,
    )(
        in_hbm(innovation.reshape(slots, tiles, cap)),
        in_hbm(inv_var.reshape(slots, tiles, cap)),
        in_hbm(obs_count.reshape(slots, tiles)),
        in_hbm(foot_block.reshape(slots, tiles, groups, cap)),
        in_hbm(foot_offset.reshape(slots, tiles, groups, cap)),
        in_hbm(weights),
        in_hbm(ens_pert),
    )
    owned = exchange(owned, "space")
    picks, hot, high = pl.pallas_call(
        lambda *refs: pick_kernel(scale, *refs),
        out_shape=(
            in_vmem((rows, LANES), F32),
            in_vmem((steps, groups * LANES, LANES), BF16),
            in_vmem((rows, LANES), jnp.int32),
        ),
        in_specs=[VMEM] * 4,
        out_specs=(VMEM,) * 3,
        scratch_shapes=[
            pltpu.VMEM((rows, LANES), jnp.int32),
            pltpu.VMEM((slots, highs, LANES), F32),
            pltpu.VMEM((slots, 2 * highs, LANES), BF16),
        ],
        compiler_params=PARAMS,
        cost_estimate=cost(4 * blocks * rows * LANES * BLOCK, 4 << 20),
    )(ens, w, fb, fo)
    joined = pl.pallas_call(
        join_kernel,
        out_shape=jax.ShapeDtypeStruct((groups, rows + steps, LANES), F32),
        in_specs=[VMEM] * 2,
        out_specs=VMEM,
        compiler_params=PARAMS,
    )(picks, owned)
    got = exchange(joined, "member")
    local = pl.pallas_call(
        gradient_kernel,
        out_shape=jax.ShapeDtypeStruct((windows, members * blocks // LANES, LANES), F32),
        in_specs=[VMEM] * 4,
        out_specs=VMEM,
        compiler_params=PARAMS,
    )(ens, got, hot, high)
    parts = exchange(local, "tm")
    return pl.pallas_call(
        lambda *refs: finish_kernel(scale, *refs),
        out_shape=jax.ShapeDtypeStruct(weights.shape, F32),
        in_specs=[VMEM] * 2,
        out_specs=VMEM,
        compiler_params=PARAMS,
    )(parts, w)


def solution(mesh):
    in_specs = (
        P("tm", "member", "space"),
        P("member", "space"),
        P("tm", "space", None, None, None),
        P("tm", "space", None, None, None),
        P("tm", "space", "member", None, None),
        P("tm", "space", "member", None, None),
        P("tm", "space", "member", None),
    )
    out_specs = P("member", "space")
    return jax.shard_map(shards, mesh=mesh, in_specs=in_specs, out_specs=out_specs, check_vma=False)
```
